32 devices in a mesh: groups: 2 (over y), segment: 4 (over z), inner: 4 (over x, core).
Axes of the slice: x: 2, y: 2, z: 4, core: 2. Of those that a mesh axis runs over, the one named last changes fastest.
Arguments:
- tokens: int32 [3, 64], P(None, 'groups'), parts along dimension 1, may hold values from 0 to 511
- embedding: bfloat16 [512, 4096], P(None, 'inner'), may hold values from -6 to 6
- in_proj: bfloat16 [4, 3, 4096, 4096], P('segment', None, None, 'inner'), may hold values from -0.09375 to 0.09375
- out_proj: bfloat16 [4, 4096, 4096], P('segment', 'inner'), may hold values from -0.09375 to 0.09375
- norm_gain: float32 [4, 4096], P('segment'), may hold values from 0.1 to 1.9
- fir_taps: float32 [4, 7, 4096], P('segment', None, 'inner'), may hold values from -2 to 2
- modal_rate: float32 [4, 8, 4096], P('segment', None, 'inner'), may hold values from 0.05 to 3
- modal_residue: float32 [4, 8, 4096], P('segment', None, 'inner'), may hold values from -2 to 2
- fir_state: float32 [4, 64, 6, 4096], P('segment', 'groups', None, 'inner'), parts along dimension 1, may hold values from -6 to 6
- modal_state: float32 [4, 64, 8, 4096], P('segment', 'groups', None, 'inner'), parts along dimension 1, may hold values from -6 to 6
- final_gain: float32 [4096], replicated, may hold values from 0.1 to 1.9
- unembed: bfloat16 [4096, 512], P(None, 'inner'), may hold values from -0.25 to 0.25
Outputs:
- logits: float32 [2, 64, 512], P(None, ('groups', 'segment'), 'inner'), parts along dimension 1
- logprob: float32 [2, 64], P(None, ('groups', 'segment')), parts along dimension 1
- fir_state_out: float32 [4, 64, 6, 4096], P('segment', 'groups', None, 'inner'), parts along dimension 1
- modal_state_out: float32 [4, 64, 8, 4096], P('segment', 'groups', None, 'inner'), parts along dimension 1
The draws below stay inside these ranges and needn't reach their ends.
There are 2 independent parts, one for each index of `groups`. The reference program is written for one: setup_inputs(seed, part) draws one part's arguments, and reference() takes and returns one part's arrays. A program takes and returns all parts, laid end to end along the dimension named above; an argument that names none is the same for every part. Nothing has to cross between parts.
All inputs are finite; a program needn't handle non-finite values.
Results may differ from the reference program's by a relative error of at most 0.025.
Values may be sent and summed in bfloat16 or wider, within the bound.
A program may use at most 128 MiB of HBM per device.

```python
import math
import jax
import jax.numpy as jnp
from jax import lax

D = 4096
VOCAB = 512
R = 8
TAPS = 7
STEPS = 2
SEQS = 32
N_SEGMENT = 4


def touch_ends(result, stream_key, least, top_value):
    longest = result.shape.index(max(result.shape))
    spots = []
    for shift in (0, 1):
        where = [jax.random.randint(jax.random.fold_in(stream_key, axis), (), 0, length) for axis, length in enumerate(result.shape)]
        where[longest] = (where[longest] + shift) % result.shape[longest]
        spots.append(tuple(where))
    return result.at[spots[0]].set(least).at[spots[1]].set(top_value)


def block_levels(own_key, dims, pieces, smallest, top_value):
    def one(position, parts):
        heights = jax.random.uniform(jax.random.fold_in(jax.random.fold_in(own_key, 6), position), (parts,), jnp.float32, smallest / len(pieces), top_value / len(pieces))
        return jnp.repeat(jnp.exp(heights), dims[position] // parts).reshape((-1,) + (1,) * (len(dims) - position - 1))

    loudness = one(*pieces[0])
    for cut in pieces[1:]:
        loudness = loudness * one(*cut)
    return loudness


def bell_draw(key, extent, width, reach, cuts=(), held_as=jnp.bfloat16):
    drawn = width * jax.random.normal(key, extent, jnp.float32)
    if cuts:
        drawn = drawn * block_levels(key, extent, cuts, -0.22, 0.18)
    return jnp.clip(drawn, -reach, reach).astype(held_as)


def setup_inputs(seed: int = 0, part: int = 0) -> dict:
    key_list = jax.random.split(jax.random.key(seed), 13)
    part_splits = jax.random.split(jax.random.fold_in(key_list[12], part), 13)
    tokens = touch_ends(jax.random.randint(part_splits[0], (STEPS + 1, SEQS), 0, VOCAB), jax.random.fold_in(part_splits[0], 1), 0, VOCAB - 1).astype(jnp.int32)
    embedding = bell_draw(key_list[1], (VOCAB, D), 1.0, 6.0, ((1, 4),))
    in_proj = bell_draw(key_list[2], (N_SEGMENT, 3, D, D), D ** -0.5, 0.09375, ((0, 4), (3, 4)))
    out_proj = bell_draw(key_list[3], (N_SEGMENT, D, D), D ** -0.5, 0.09375, ((0, 4), (1, 4)))
    norm_gain = jnp.clip(1.0 + 0.18 * jax.random.normal(key_list[4], (N_SEGMENT, D), jnp.float32), 0.1, 1.9)
    fir_taps = bell_draw(key_list[5], (N_SEGMENT, TAPS, D), TAPS ** -0.5, 2.0, ((0, 4), (2, 4)), jnp.float32)
    modal_rate = jnp.clip(jnp.exp(math.log(3.0) - 4.0943445 * jax.random.uniform(key_list[6], (N_SEGMENT, R, D), jnp.float32) ** block_levels(key_list[6], (N_SEGMENT, R, D), ((0, 4), (2, 4)), -0.2, 0.2)), 0.05, 3.0)
    modal_residue = bell_draw(key_list[7], (N_SEGMENT, R, D), R ** -0.5, 2.0, ((0, 4), (2, 4)), jnp.float32)
    fir_state = bell_draw(part_splits[8], (N_SEGMENT, SEQS, TAPS - 1, D), 1.0, 6.0, ((0, 4), (3, 4)), jnp.float32)
    modal_state = bell_draw(part_splits[9], (N_SEGMENT, SEQS, R, D), 1.0, 6.0, ((0, 4), (3, 4)), jnp.float32)
    final_gain = jnp.clip(1.0 + 0.18 * jax.random.normal(key_list[10], (D,), jnp.float32), 0.1, 1.9)
    unembed = bell_draw(key_list[11], (D, VOCAB), (D // 9) ** -0.5, 0.25, ((1, 4),))
    return dict(tokens=tokens, embedding=embedding, in_proj=in_proj, out_proj=out_proj, norm_gain=norm_gain, fir_taps=fir_taps, modal_rate=modal_rate, modal_residue=modal_residue, fir_state=fir_state, modal_state=modal_state, final_gain=final_gain, unembed=unembed)


def normed(values, scale_gain):
    mean_square = lax.optimization_barrier(jnp.mean(values * values, axis=-1, keepdims=True))
    return values * lax.rsqrt(mean_square + 1e-05) * scale_gain

def reference(tokens, embedding, in_proj, out_proj, norm_gain, fir_taps, modal_rate, modal_residue, fir_state, modal_state, final_gain, unembed):
    fir_list = [fir_state[layer_index] for layer_index in range(N_SEGMENT)]
    modal_list = [modal_state[layer_index] for layer_index in range(N_SEGMENT)]
    finals = []
    for step_index in range(STEPS):
        stream = jnp.take(embedding, tokens[step_index], axis=0)
        for layer_index in range(N_SEGMENT):
            normalized = normed(stream.astype(jnp.float32), norm_gain[layer_index]).astype(jnp.bfloat16)
            projected = jnp.einsum('bd,jdc->jbc', normalized.astype(jnp.float32), in_proj[layer_index].astype(jnp.float32))
            query_part = projected[0]
            product = projected[1] * projected[2]
            taps_now = fir_taps[layer_index]
            if layer_index % 2 == 0:
                window = jnp.concatenate([fir_list[layer_index], product[:, None, :]], axis=1)
                filtered = lax.optimization_barrier(jnp.sum(window * taps_now[::-1][None], axis=1))
                fir_list[layer_index] = window[:, 1:]
            else:
                decay_factor = jnp.exp(-modal_rate[layer_index])
                mode_values = decay_factor[None] * modal_list[layer_index] + (1.0 - decay_factor[None]) * product[:, None, :]
                filtered = lax.optimization_barrier(jnp.sum(modal_residue[layer_index][None] * mode_values, axis=1)) + taps_now[0][None] * product
                modal_list[layer_index] = mode_values
            gated_rows = (query_part * filtered).astype(jnp.bfloat16)
            mixed_sum = jnp.dot(gated_rows, out_proj[layer_index], preferred_element_type=jnp.float32)
            stream = (stream.astype(jnp.float32) + mixed_sum).astype(jnp.bfloat16)
        finals.append(stream)
    final_stream = jnp.stack(finals)
    head_in = normed(final_stream.astype(jnp.float32), final_gain).astype(jnp.bfloat16)
    logits = jnp.einsum('tsd,dv->tsv', head_in.astype(jnp.float32), unembed.astype(jnp.float32))
    log_total = jnp.log(lax.optimization_barrier(jnp.sum(jnp.exp(logits), axis=-1)))
    target = jnp.take_along_axis(logits, tokens[1:][..., None], axis=-1)[..., 0]
    return (logits, target - log_total, jnp.stack(fir_list), jnp.stack(modal_list))
```

```python
import functools

import jax
import jax.numpy as jnp
from jax import lax
from jax.experimental import pallas as pl
from jax.experimental.pallas import tpu as pltpu
from jax.sharding import PartitionSpec as P

EPS = 1e-05
MESH = pl.DeviceIdType.MESH
F32 = jnp.float32
BF16 = jnp.bfloat16


def column_of(row, first, count):
    length = row.shape[1]
    down = lax.broadcasted_iota(jnp.int32, (count, length), 0) + first
    across = lax.broadcasted_iota(jnp.int32, (count, length), 1)
    picked = jnp.where(down == across, jnp.broadcast_to(row, (count, length)), 0.0)
    return jnp.sum(picked, axis=1, keepdims=True)


def kernel(
    pieces, inner, segments,
    tokens, norm_gain, final_gain, taps, rate, residue,
    embedding, w_in, w_out, fir_state, modal_state, unembed,
    logits_out, logprob_out, product_out,
    emb_v, in_v, out_v, fir_v, modal_v, unembed_v,
    xbuf, fbuf, sbuf, rbuf, zbuf, acc, squares, state_part, gated,
    head_acc, scatter, lbuf, ebuf,
    emb_sem, in_sem, out_sem, state_sem, unembed_sem,
    x_send, x_recv, r_send, r_recv, z_send, f_send, f_recv, l_send, l_recv, e_send, e_recv,
):
    seg = lax.axis_index("segment")
    me = lax.axis_index("inner")
    last = segments - 1
    steps = tokens.shape[0] - 1
    seqs = tokens.shape[1]
    rows = steps * seqs
    width = emb_v.shape[1]
    sub = width // pieces
    vocab = emb_v.shape[0]
    vocab_local = unembed.shape[1]
    block = seqs // segments
    depth = fir_v.shape[1]
    full = inner * width
    is_short = seg % 2 == 0

    def peer(p):
        return (me // 2 + p // 2) % (inner // 2) * 2 + (me + p) % 2

    barrier = pltpu.get_barrier_semaphore()
    for p in range(1, inner):
        pl.semaphore_signal(barrier, inc=1, device_id={"inner": peer(p)}, device_id_type=MESH)
    for d in range(1, segments):
        pl.semaphore_signal(
            barrier, inc=1, device_id={"segment": (seg + d) % segments}, device_id_type=MESH
        )

    def emb_copy():
        return pltpu.make_async_copy(embedding, emb_v, emb_sem)

    def fir_copy():
        return pltpu.make_async_copy(fir_state.at[0], fir_v, state_sem)

    def modal_copy():
        return pltpu.make_async_copy(modal_state.at[0], modal_v, state_sem)

    def in_copy(k, q):
        return pltpu.make_async_copy(
            w_in.at[0, :, pl.ds(pl.multiple_of(q * width + k * sub, sub), sub), :],
            in_v.at[q * pieces + k],
            in_sem.at[q * pieces + k],
        )

    def out_copy(k, q):
        return pltpu.make_async_copy(
            w_out.at[0, :, pl.ds(pl.multiple_of(q * width + k * sub, sub), sub)],
            out_v.at[q * pieces + k],
            out_sem.at[q * pieces + k],
        )

    def unembed_copy():
        return pltpu.make_async_copy(unembed, unembed_v, unembed_sem)

    @pl.when(seg == 0)
    def _():
        emb_copy().start()

    @pl.when(is_short)
    def _():
        fir_copy().start()

    @pl.when(jnp.logical_not(is_short))
    def _():
        modal_copy().start()

    @pl.loop(0, pieces)
    def _(k):
        in_copy(k, me).start()

    @pl.loop(0, pieces * (inner - 1))
    def _(t):
        in_copy(t // (inner - 1), peer(t % (inner - 1) + 1)).start()

    @pl.loop(0, pieces * inner)
    def _(t):
        out_copy(t // inner, peer((t + 1) % inner)).start()

    unembed_copy().start()
    pl.semaphore_wait(barrier, inner - 1 + segments - 1)

    def x_copy(k, p):
        return pltpu.make_async_remote_copy(
            src_ref=xbuf.at[k * inner + me],
            dst_ref=xbuf.at[k * inner + me],
            send_sem=x_send.at[k * inner + p],
            recv_sem=x_recv.at[k * inner + me],
            device_id={"inner": peer(p)},
            device_id_type=MESH,
        )

    def x_arrival(k, q):
        return pltpu.make_async_copy(
            xbuf.at[k * inner + q], xbuf.at[k * inner + q], x_recv.at[k * inner + q]
        )

    def x_forward(k):
        for p in range(inner - 1, 0, -1):
            x_copy(k, p).start()

    @pl.when(seg == 0)
    def _():
        emb_copy().wait()
        for k in range(pieces):
            for t in range(steps):
                ids = column_of(tokens[pl.ds(t, 1), :].astype(F32), 0, seqs)
                ids = ids.astype(jnp.int32)
                hot = lax.broadcasted_iota(jnp.int32, (seqs, vocab), 1) == ids
                hot = hot.astype(F32).astype(BF16)
                looked_up = jnp.dot(
                    hot, emb_v[:, k * sub:(k + 1) * sub], preferred_element_type=F32
                )
                xbuf[k * inner + me, t * seqs:(t + 1) * seqs, :] = looked_up.astype(BF16)
            x_forward(k)

    @pl.when(is_short)
    def _():
        fir_copy().wait()

        @pl.loop(0, seqs)
        def _(b):
            rows_b = fir_v[b]
            for t in range(steps):
                total = jnp.zeros((1, width), F32)
                for i in range(depth - t):
                    total = total + rows_b[i + t:i + t + 1, :] * taps[0, depth - i:depth - i + 1, :]
                state_part[t, pl.ds(b, 1), :] = total

    @pl.when(jnp.logical_not(is_short))
    def _():
        modal_copy().wait()
        decay = jnp.exp(-rate[0])

        @pl.loop(0, seqs)
        def _(b):
            value = modal_v[b]
            for t in range(steps):
                value = value * decay
                state_part[t, pl.ds(b, 1), :] = jnp.sum(value * residue[0], axis=0, keepdims=True)

    acc[...] = jnp.zeros_like(acc)
    squares[...] = jnp.zeros_like(squares)

    def consume(k, q):
        values = xbuf[k * inner + q].astype(F32)
        total = squares[...]
        for c in range(sub // 128):
            piece = values[:, c * 128:(c + 1) * 128]
            total = total + piece * piece
        squares[...] = total
        offset = pl.multiple_of(q * width + k * sub, sub)
        scaled = (values * norm_gain[:, pl.ds(offset, sub)]).astype(BF16)
        in_copy(k, q).wait()
        for j in range(3):
            acc[j] += jnp.dot(scaled, in_v[q * pieces + k, j], preferred_element_type=F32)

    @pl.loop(0, pieces)
    def _(k):
        @pl.when(seg > 0)
        def _():
            x_arrival(k, me).wait()
            x_forward(k)

        consume(k, me)

    @pl.loop(0, pieces * (inner - 1))
    def _(t):
        k = t // (inner - 1)
        q = peer(t % (inner - 1) + 1)
        x_arrival(k, q).wait()
        consume(k, q)

    scale = lax.rsqrt(jnp.sum(squares[...], axis=1, keepdims=True) / full + EPS)

    decay_all = jnp.exp(-rate[0])
    coefs = []
    power = jnp.ones_like(decay_all)
    for m in range(steps):
        modal_coef = jnp.sum(residue[0] * power * (1.0 - decay_all), axis=0, keepdims=True)
        if m == 0:
            modal_coef = modal_coef + taps[0, 0:1, :]
        power = power * decay_all
        short_coef = taps[0, m:m + 1, :] if m <= depth else jnp.zeros((1, width), F32)
        coefs.append(jnp.where(is_short, short_coef, modal_coef))
    for c in range(0, width, sub):
        cols = slice(c, c + sub)
        products = []
        for t in range(steps):
            part = slice(t * seqs, (t + 1) * seqs)
            scale_t = scale[part]
            product = (acc[1, part, cols] * scale_t) * (acc[2, part, cols] * scale_t)
            products.append(product)
            product_out[t, :, cols] = product
            filtered = state_part[t, :, cols]
            for u in range(t + 1):
                filtered = filtered + coefs[t - u][:, cols] * products[u]
            gated[part, cols] = (acc[0, part, cols] * scale_t * filtered).astype(BF16)

    def r_copy(k, p):
        q = peer(p)
        return pltpu.make_async_remote_copy(
            src_ref=sbuf.at[k * inner + q],
            dst_ref=rbuf.at[k * inner + me],
            send_sem=r_send.at[k * inner + p],
            recv_sem=r_recv.at[k * inner + me],
            device_id={"inner": q},
            device_id_type=MESH,
        )

    def r_arrival(k, q):
        return pltpu.make_async_copy(
            rbuf.at[k * inner + q], rbuf.at[k * inner + q], r_recv.at[k * inner + q]
        )

    def z_copy(k):
        return pltpu.make_async_remote_copy(
            src_ref=zbuf.at[k],
            dst_ref=xbuf.at[k * inner + me],
            send_sem=z_send.at[k],
            recv_sem=x_recv.at[k * inner + me],
            device_id={"segment": (seg + 1) % segments},
            device_id_type=MESH,
        )

    def f_copy(k, p):
        return pltpu.make_async_remote_copy(
            src_ref=zbuf.at[k],
            dst_ref=fbuf.at[k * inner + me],
            send_sem=f_send.at[k * inner + p],
            recv_sem=f_recv.at[k * inner + me],
            device_id={"inner": peer(p)},
            device_id_type=MESH,
        )

    def f_arrival(k, q):
        return pltpu.make_async_copy(
            fbuf.at[k * inner + q], fbuf.at[k * inner + q], f_recv.at[k * inner + q]
        )

    @pl.loop(0, pieces)
    def _(k):
        @pl.loop(1, inner)
        def _(p):
            q = peer(inner - p)
            out_copy(k, q).wait()
            sbuf[k * inner + q] = jnp.dot(
                gated[...], out_v[q * pieces + k], preferred_element_type=F32
            ).astype(BF16)
            r_copy(k, inner - p).start()

        out_copy(k, me).wait()
        acc[0, :, pl.ds(pl.multiple_of(k * sub, sub), sub)] = jnp.dot(
            gated[...], out_v[me * pieces + k], preferred_element_type=F32
        )

    @pl.loop(0, pieces)
    def _(k):
        total = acc[0, :, pl.ds(pl.multiple_of(k * sub, sub), sub)]
        for p in range(1, inner):
            q = peer(p)
            r_arrival(k, q).wait()
            total = total + rbuf[k * inner + q].astype(F32)
        zbuf[k] = (total + xbuf[k * inner + me].astype(F32)).astype(BF16)

        @pl.when(seg < last)
        def _():
            z_copy(k).start()

        @pl.when(seg == last)
        def _():
            for p in range(inner - 1, 0, -1):
                f_copy(k, p).start()

    unembed_copy().wait()

    def l_copy(s):
        return pltpu.make_async_remote_copy(
            src_ref=scatter.at[s],
            dst_ref=lbuf,
            send_sem=l_send.at[s],
            recv_sem=l_recv,
            device_id={"segment": s},
            device_id_type=MESH,
        )

    @pl.when(seg == last)
    def _():
        head_acc[...] = jnp.zeros_like(head_acc)
        squares[...] = jnp.zeros_like(squares)

        def take(k, q, chunk):
            values = chunk.astype(F32)
            total = squares[...]
            for c in range(sub // 128):
                piece = values[:, c * 128:(c + 1) * 128]
                total = total + piece * piece
            squares[...] = total
            offset = pl.multiple_of(q * width + k * sub, sub)
            scaled = (values * final_gain[:, pl.ds(offset, sub)]).astype(BF16)
            head_acc[:, :vocab_local] += jnp.dot(
                scaled, unembed_v[pl.ds(offset, sub), :], preferred_element_type=F32
            )

        @pl.loop(0, pieces)
        def _(k):
            take(k, me, zbuf[k])

        @pl.loop(0, pieces * (inner - 1))
        def _(t):
            k = t // (inner - 1)
            q = peer(t % (inner - 1) + 1)
            f_arrival(k, q).wait()
            take(k, q, fbuf[k * inner + q])

        final_scale = lax.rsqrt(jnp.sum(squares[...], axis=1, keepdims=True) / full + EPS)
        logits = head_acc[...] * final_scale
        for s in range(segments):
            for t in range(steps):
                start = t * seqs + s * block
                if s < last:
                    scatter[s, t] = logits[start:start + block]
                else:
                    lbuf[t] = logits[start:start + block]
            if s < last:
                l_copy(s).start()

    @pl.when(seg < last)
    def _():
        pltpu.make_async_copy(lbuf, lbuf, l_recv).wait()

    def e_copy(p):
        return pltpu.make_async_remote_copy(
            src_ref=ebuf.at[me],
            dst_ref=ebuf.at[me],
            send_sem=e_send.at[p],
            recv_sem=e_recv.at[me],
            device_id={"inner": peer(p)},
            device_id_type=MESH,
        )

    columns = lax.broadcasted_iota(jnp.int32, (block, vocab_local), 1) + me * vocab_local
    lanes = lax.broadcasted_iota(jnp.int32, (block, 128), 1)
    for t in range(steps):
        logits_t = lbuf[t, :, :vocab_local]
        logits_out[t] = logits_t
        target = column_of(tokens[pl.ds(t + 1, 1), :].astype(F32), seg * block, block)
        hit = columns == target.astype(jnp.int32)
        exp_sum = jnp.sum(jnp.exp(logits_t), axis=1, keepdims=True)
        target_part = jnp.sum(jnp.where(hit, logits_t, 0.0), axis=1, keepdims=True)
        ebuf[me, t] = jnp.where(lanes == 0, exp_sum, target_part)
    for p in range(inner - 1, 0, -1):
        e_copy(p).start()
    sums = ebuf[me]
    for p in range(1, inner):
        q = peer(p)
        pltpu.make_async_copy(ebuf.at[q], ebuf.at[q], e_recv.at[q]).wait()
        sums = sums + ebuf[q]
    for t in range(steps):
        logprob_out[t] = sums[t, :, 1:2] - jnp.log(sums[t, :, 0:1])

    @pl.loop(0, pieces)
    def _(k):
        for p in range(1, inner):
            x_copy(k, p).wait_send()
            r_copy(k, p).wait_send()

        @pl.when(seg < last)
        def _():
            z_copy(k).wait_send()

        @pl.when(seg == last)
        def _():
            for p in range(1, inner):
                f_copy(k, p).wait_send()

    @pl.when(seg == last)
    def _():
        for s in range(segments - 1):
            l_copy(s).wait_send()

    for p in range(1, inner):
        e_copy(p).wait_send()


def per_device(
    inner, segments, tokens, embedding, in_proj, out_proj, norm_gain, fir_taps, modal_rate,
    modal_residue, fir_state, modal_state, final_gain, unembed,
):
    steps = tokens.shape[0] - 1
    seqs = tokens.shape[1]
    rows = steps * seqs
    vocab, width = embedding.shape
    pieces = max(1, width // 256)
    sub = width // pieces
    full = inner * width
    vocab_local = unembed.shape[1]
    padded = max(128, vocab_local)
    block = seqs // segments
    whole = pl.BlockSpec(memory_space=pltpu.VMEM)
    anywhere = pl.BlockSpec(memory_space=pl.ANY)
    dma = pltpu.SemaphoreType.DMA
    logits, logprob, product = pl.pallas_call(
        functools.partial(kernel, pieces, inner, segments),
        out_shape=(
            jax.ShapeDtypeStruct((steps, block, vocab_local), F32),
            jax.ShapeDtypeStruct((steps, block, 1), F32),
            jax.ShapeDtypeStruct((steps, seqs, width), F32),
        ),
        in_specs=[whole] * 6 + [anywhere] * 6,
        out_specs=(whole, whole, whole),
        scratch_shapes=[
            pltpu.VMEM((vocab, width), BF16),
            pltpu.VMEM((inner * pieces, 3, sub, width), BF16),
            pltpu.VMEM((inner * pieces, width, sub), BF16),
            pltpu.VMEM(fir_state.shape[1:], F32),
            pltpu.VMEM(modal_state.shape[1:], F32),
            pltpu.VMEM((full, vocab_local), BF16),
            pltpu.VMEM((pieces * inner, rows, sub), BF16),
            pltpu.VMEM((pieces * inner, rows, sub), BF16),
            pltpu.VMEM((pieces * inner, rows, sub), BF16),
            pltpu.VMEM((pieces * inner, rows, sub), BF16),
            pltpu.VMEM((pieces, rows, sub), BF16),
            pltpu.VMEM((3, rows, width), F32),
            pltpu.VMEM((rows, 128), F32),
            pltpu.VMEM((steps, seqs, width), F32),
            pltpu.VMEM((rows, width), BF16),
            pltpu.VMEM((rows, padded), F32),
            pltpu.VMEM((segments, steps, block, padded), F32),
            pltpu.VMEM((steps, block, padded), F32),
            pltpu.VMEM((inner, steps, block, 128), F32),
            dma,
            dma((inner * pieces,)),
            dma((inner * pieces,)),
            dma,
            dma,
            dma((pieces * inner,)),
            dma((pieces * inner,)),
            dma((pieces * inner,)),
            dma((pieces * inner,)),
            dma((pieces,)),
            dma((pieces * inner,)),
            dma((pieces * inner,)),
            dma((segments,)),
            dma,
            dma((inner,)),
            dma((inner,)),
        ],
        compiler_params=pltpu.CompilerParams(
            collective_id=0, has_side_effects=True, vmem_limit_bytes=52 * 1024 * 1024
        ),
    )(
        tokens, norm_gain, final_gain[None], fir_taps, modal_rate, modal_residue,
        embedding, in_proj, out_proj, fir_state, modal_state, unembed,
    )
    is_short = lax.axis_index("segment") % 2 == 0
    newest = jnp.transpose(product, (1, 0, 2))
    depth = fir_state.shape[2]
    shifted = jnp.concatenate([fir_state[0], newest], axis=1)[:, steps:]
    decay = jnp.exp(-modal_rate[0])[None]
    mode_values = modal_state[0]
    for t in range(steps):
        mode_values = decay * mode_values + (1.0 - decay) * product[t][:, None, :]
    fir_out = jnp.where(is_short, shifted, fir_state[0])
    modal_out = jnp.where(is_short, modal_state[0], mode_values)
    return (logits, logprob[..., 0], fir_out[None], modal_out[None])


def solution(mesh):
    inner = mesh.shape["inner"]
    segments = mesh.shape["segment"]
    return jax.shard_map(
        functools.partial(per_device, inner, segments),
        mesh=mesh,
        in_specs=(
            P(None, "groups"),
            P(None, "inner"),
            P("segment", None, None, "inner"),
            P("segment", "inner", None),
            P("segment", None),
            P("segment", None, "inner"),
            P("segment", None, "inner"),
            P("segment", None, "inner"),
            P("segment", "groups", None, "inner"),
            P("segment", "groups", None, "inner"),
            P(),
            P(None, "inner"),
        ),
        out_specs=(
            P(None, ("groups", "segment"), "inner"),
            P(None, ("groups", "segment")),
            P("segment", "groups", None, "inner"),
            P("segment", "groups", None, "inner"),
        ),
        check_vma=False,
    )
```

```python
import functools

import jax
import jax.numpy as jnp
from jax import lax
from jax.experimental import pallas as pl
from jax.experimental.pallas import tpu as pltpu
from jax.sharding import PartitionSpec as P

EPS = 1e-05
MESH = pl.DeviceIdType.MESH
F32 = jnp.float32
BF16 = jnp.bfloat16


def column_of(row, first, count):
    length = row.shape[1]
    down = lax.broadcasted_iota(jnp.int32, (count, length), 0) + first
    across = lax.broadcasted_iota(jnp.int32, (count, length), 1)
    picked = jnp.where(down == across, jnp.broadcast_to(row, (count, length)), 0.0)
    return jnp.sum(picked, axis=1, keepdims=True)


def kernel(
    pieces, inner, segments,
    tokens_h, norm_gain_h, final_gain_h, taps_h, rate_h, residue_h,
    embedding, w_in, w_out, fir_state, modal_state, unembed,
    packed_out, product_out,
    product_v, tokens, norm_gain, final_gain, taps, rate, residue,
    emb_v, in_v, out_v, fir_v, modal_v, unembed_v,
    xbuf, fbuf, abuf, arbuf, bbuf, brbuf, zbuf, acc, mixed, squares, state_part, coefs, gated,
    head_acc, scatter, lbuf, ebuf,
    product_sem, small_sem, emb_sem, in_sem, out_sem, state_sem, unembed_sem,
    x_send, x_recv, a_send, a_recv, b_send, b_recv, z_send, f_send, f_recv,
    l_send, l_recv, e_send, e_recv,
):
    seg = lax.axis_index("segment")
    me = lax.axis_index("inner")
    last = segments - 1
    chips = inner // 2
    chip = me // 2
    core = me % 2
    steps = tokens.shape[0] - 1
    seqs = tokens.shape[1]
    rows = steps * seqs
    width = emb_v.shape[1]
    sub = width // pieces
    vocab = emb_v.shape[0]
    vocab_local = unembed.shape[1]
    padded = lbuf.shape[2]
    block = seqs // segments
    depth = fir_v.shape[0]
    full = inner * width
    is_short = seg % 2 == 0
    sibling = chip * 2 + (core + 1) % 2

    def member(dx, dc):
        return (chip + dx) % chips * 2 + (core + dc) % 2

    def remote(src, dst, send, recv, where):
        return pltpu.make_async_remote_copy(
            src_ref=src, dst_ref=dst, send_sem=send, recv_sem=recv,
            device_id=where, device_id_type=MESH,
        )

    def arrival(ref, sem):
        pltpu.make_async_copy(ref, ref, sem).wait()

    barrier = pltpu.get_barrier_semaphore()
    for p in range(1, inner):
        pl.semaphore_signal(
            barrier, inc=1, device_id={"inner": member(p // 2, p % 2)}, device_id_type=MESH
        )
    for d in range(1, segments):
        pl.semaphore_signal(
            barrier, inc=1, device_id={"segment": (seg + d) % segments}, device_id_type=MESH
        )

    emb_copy = pltpu.make_async_copy(embedding, emb_v, emb_sem)
    fir_copy = pltpu.make_async_copy(fir_state.at[0], fir_v, state_sem)
    modal_copy = pltpu.make_async_copy(modal_state.at[0], modal_v, state_sem)
    unembed_copy = pltpu.make_async_copy(unembed, unembed_v, unembed_sem)
    small = [
        pltpu.make_async_copy(source, target, small_sem.at[index])
        for index, (source, target) in enumerate((
            (tokens_h, tokens), (taps_h, taps), (rate_h, rate), (residue_h, residue),
            (norm_gain_h, norm_gain), (final_gain_h, final_gain),
        ))
    ]

    def in_copy(q, j):
        return pltpu.make_async_copy(
            w_in.at[0, j, pl.ds(pl.multiple_of(q * width, width), width), :],
            in_v.at[q, j],
            in_sem.at[q * 3 + j],
        )

    def out_copy(q, k):
        return pltpu.make_async_copy(
            w_out.at[0, :, pl.ds(pl.multiple_of(q * width + k * sub, sub), sub)],
            out_v.at[q * pieces + k],
            out_sem.at[q * pieces + k],
        )

    small[0].start()

    @pl.when(seg == 0)
    def _():
        emb_copy.start()

    for copy in small[1:]:
        copy.start()

    @pl.when(is_short)
    def _():
        fir_copy.start()

    @pl.when(jnp.logical_not(is_short))
    def _():
        modal_copy.start()

    @pl.loop(0, inner)
    def _(t):
        q = member(t % chips, t // chips)
        for j in range(3):
            in_copy(q, j).start()

    for dc in (1, 0):
        @pl.loop(0, pieces * chips)
        def _(t):
            out_copy(member(t % chips, dc), t // chips).start()

    unembed_copy.start()
    small[0].wait()

    def gather_copy(buf, source, send, recv, k, dx):
        where = sibling if dx == 0 else member(dx, 0)
        return remote(
            source, buf.at[me * pieces + k], send.at[dx * pieces + k],
            recv.at[me * pieces + k], {"inner": where},
        )

    def hand_on(buf, send, recv, k, dx):
        q = member(dx, 0)
        return remote(
            buf.at[q * pieces + k], buf.at[q * pieces + k],
            send.at[(chips + dx) * pieces + k], recv.at[q * pieces + k], {"inner": sibling},
        )

    def x_copy(k, dx):
        return gather_copy(xbuf, xbuf.at[me * pieces + k], x_send, x_recv, k, dx)

    def f_copy(k, dx):
        return gather_copy(fbuf, zbuf.at[k], f_send, f_recv, k, dx)

    def spread(copy_of, k):
        for dx in range(chips - 1, -1, -1):
            copy_of(k, dx).start()

    def pass_on(buf, send, recv):
        for k in range(pieces):
            for dx in range(1, chips):
                q = member(dx, 0)
                arrival(buf.at[q * pieces + k], recv.at[q * pieces + k])
                hand_on(buf, send, recv, k, dx).start()

    @pl.when(seg == 0)
    def _():
        ids = jnp.concatenate(
            [column_of(tokens[pl.ds(t, 1), :].astype(F32), 0, seqs) for t in range(steps)], axis=0
        ).astype(jnp.int32)
        hot = lax.broadcasted_iota(jnp.int32, (rows, vocab), 1) == ids
        hot = hot.astype(F32).astype(BF16)
        emb_copy.wait()
        for k in range(pieces):
            looked_up = jnp.dot(
                hot, emb_v[:, k * sub:(k + 1) * sub], preferred_element_type=F32
            )
            xbuf[me * pieces + k] = looked_up.astype(BF16)

    pl.semaphore_wait(barrier, inner - 1 + segments - 1)

    @pl.when(seg == 0)
    def _():
        for k in range(pieces):
            spread(x_copy, k)

    for copy in small[1:]:
        copy.wait()

    acc[...] = jnp.zeros_like(acc)
    squares[...] = jnp.zeros_like(squares)

    @pl.when(is_short)
    def _():
        fir_copy.wait()
        for t in range(steps):
            coefs[t] = taps[t] if t <= depth else jnp.zeros((1, width), F32)
            for c in range(0, width, 256):
                cols = slice(c, c + 256)
                total = jnp.zeros((seqs, 256), F32)
                for i in range(depth - t):
                    total = total + fir_v[i + t, :, cols] * taps[depth - i, :, cols]
                state_part[t, :, cols] = total

    @pl.when(jnp.logical_not(is_short))
    def _():
        decay = jnp.exp(-rate[0])
        weight = residue[0] * (1.0 - decay)
        for t in range(steps):
            coef = jnp.sum(weight, axis=0, keepdims=True)
            coefs[t] = coef + taps[0] if t == 0 else coef
            weight = weight * decay
        modal_copy.wait()

        @pl.loop(0, seqs)
        def _(b):
            value = modal_v[b]
            for t in range(steps):
                value = value * decay
                state_part[t, pl.ds(b, 1), :] = jnp.sum(value * residue[0], axis=0, keepdims=True)

    def take(values, gain):
        values = values.astype(F32)
        total = squares[...]
        for c in range(0, width, 128):
            piece = values[:, c:c + 128]
            total = total + piece * piece
        squares[...] = total
        return (values * gain).astype(BF16)

    def block_of(buf, q):
        return jnp.concatenate([buf[q * pieces + k] for k in range(pieces)], axis=1)

    @pl.when(seg > 0)
    def _():
        for k in range(pieces):
            arrival(xbuf.at[me * pieces + k], x_recv.at[me * pieces + k])
            spread(x_copy, k)

    @pl.loop(0, inner)
    def _(t):
        q = member(t % chips, t // chips)

        @pl.when(t == 1)
        def _():
            pass_on(xbuf, x_send, x_recv)

        @pl.when(t >= chips)
        def _():
            for k in range(pieces):
                arrival(xbuf.at[q * pieces + k], x_recv.at[q * pieces + k])

        offset = pl.multiple_of(q * width, width)
        scaled = take(block_of(xbuf, q), norm_gain[:, pl.ds(offset, width)])
        for j in range(3):
            in_copy(q, j).wait()
            acc[j] += jnp.dot(scaled, in_v[q, j], preferred_element_type=F32)

    scale = lax.rsqrt(jnp.sum(squares[...], axis=1, keepdims=True) / full + EPS)
    for c in range(0, width, sub):
        cols = slice(c, c + sub)
        products = []
        for t in range(steps):
            part = slice(t * seqs, (t + 1) * seqs)
            scale_t = scale[part]
            product = (acc[1, part, cols] * scale_t) * (acc[2, part, cols] * scale_t)
            products.append(product)
            product_v[t, :, cols] = product
            filtered = state_part[t, :, cols]
            for u in range(t + 1):
                filtered = filtered + coefs[t - u, :, cols] * products[u]
            gated[part, cols] = (acc[0, part, cols] * scale_t * filtered).astype(BF16)

    product_copy = pltpu.make_async_copy(product_v, product_out, product_sem)
    product_copy.start()

    def a_copy(k):
        return remote(abuf.at[k], arbuf.at[k], a_send.at[k], a_recv.at[k], {"inner": sibling})

    def b_copy(k, dx):
        return remote(
            bbuf.at[dx * pieces + k], brbuf.at[chip * pieces + k], b_send.at[dx * pieces + k],
            b_recv.at[chip * pieces + k], {"inner": member(dx, 0)},
        )

    def z_copy(k):
        return remote(
            zbuf.at[k], xbuf.at[me * pieces + k], z_send.at[k],
            x_recv.at[me * pieces + k], {"segment": (seg + 1) % segments},
        )

    def mix(q, k):
        out_copy(q, k).wait()
        return jnp.dot(gated[...], out_v[q * pieces + k], preferred_element_type=F32)

    @pl.loop(0, pieces)
    def _(k):
        @pl.loop(0, chips)
        def _(x):
            abuf[k, x] = mix(x * 2 + (core + 1) % 2, k).astype(BF16)

        a_copy(k).start()

    @pl.loop(0, pieces)
    def _(k):
        for dx in range(chips - 1, -1, -1):
            mixed[dx] = mix(member(dx, 0), k)
        arrival(arbuf.at[k], a_recv.at[k])
        for dx in range(chips - 1, 0, -1):
            total = mixed[dx] + arbuf[k, (chip + dx) % chips].astype(F32)
            bbuf[dx * pieces + k] = total.astype(BF16)
            b_copy(k, dx).start()
        total = mixed[0] + arbuf[k, chip].astype(F32)
        acc[0, :, pl.ds(pl.multiple_of(k * sub, sub), sub)] = (
            total + xbuf[me * pieces + k].astype(F32)
        )

    @pl.loop(0, pieces)
    def _(k):
        total = acc[0, :, pl.ds(pl.multiple_of(k * sub, sub), sub)]
        for dx in range(1, chips):
            source = (chip + dx) % chips * pieces + k
            arrival(brbuf.at[source], b_recv.at[source])
            total = total + brbuf[source].astype(F32)
        zbuf[k] = total.astype(BF16)

        @pl.when(seg < last)
        def _():
            z_copy(k).start()

        @pl.when(seg == last)
        def _():
            spread(f_copy, k)

    unembed_copy.wait()

    def l_copy(s):
        return remote(scatter.at[s], lbuf, l_send.at[s], l_recv, {"segment": s})

    @pl.when(seg == last)
    def _():
        squares[...] = jnp.zeros_like(squares)
        head_acc[...] = jnp.zeros_like(head_acc)

        def head(values, q):
            offset = pl.multiple_of(q * width, width)
            scaled = take(values, final_gain[:, pl.ds(offset, width)])
            head_acc[:, :vocab_local] += jnp.dot(
                scaled, unembed_v[pl.ds(offset, width), :], preferred_element_type=F32
            )

        head(jnp.concatenate([zbuf[k] for k in range(pieces)], axis=1), me)
        pass_on(fbuf, f_send, f_recv)

        @pl.loop(1, inner)
        def _(t):
            q = member(t % chips, t // chips)

            @pl.when(t >= chips)
            def _():
                for k in range(pieces):
                    arrival(fbuf.at[q * pieces + k], f_recv.at[q * pieces + k])

            head(block_of(fbuf, q), q)

        final_scale = lax.rsqrt(jnp.sum(squares[...], axis=1, keepdims=True) / full + EPS)
        logits = head_acc[...] * final_scale
        for s in range(segments):
            for t in range(steps):
                start = t * seqs + s * block
                if s < last:
                    scatter[s, t] = logits[start:start + block]
                else:
                    lbuf[t] = logits[start:start + block]
            if s < last:
                l_copy(s).start()

    @pl.when(seg < last)
    def _():
        arrival(lbuf, l_recv)

    def e_copy(p):
        return remote(
            ebuf.at[me], ebuf.at[me], e_send.at[p], e_recv.at[me],
            {"inner": member(p // 2, p % 2)},
        )

    columns = lax.broadcasted_iota(jnp.int32, (block, vocab_local), 1) + me * vocab_local
    lanes = lax.broadcasted_iota(jnp.int32, (block, 128), 1)
    for t in range(steps):
        logits_t = lbuf[t, :, :vocab_local]
        packed_out[t, :, :vocab_local] = logits_t
        target = column_of(tokens[pl.ds(t + 1, 1), :].astype(F32), seg * block, block)
        hit = columns == target.astype(jnp.int32)
        exp_sum = jnp.sum(jnp.exp(logits_t), axis=1, keepdims=True)
        target_part = jnp.sum(jnp.where(hit, logits_t, 0.0), axis=1, keepdims=True)
        ebuf[me, t] = jnp.where(lanes == 0, exp_sum, target_part)
    for p in range(inner - 1, 0, -1):
        e_copy(p).start()
    sums = ebuf[me]
    for p in range(1, inner):
        q = member(p // 2, p % 2)
        arrival(ebuf.at[q], e_recv.at[q])
        sums = sums + ebuf[q]
    for t in range(steps):
        logprob = sums[t, :, 1:2] - jnp.log(sums[t, :, 0:1])
        packed_out[t, :, padded:] = jnp.broadcast_to(logprob, (block, 128))

    product_copy.wait()

    @pl.loop(0, pieces)
    def _(k):
        a_copy(k).wait_send()
        for dx in range(chips):
            x_copy(k, dx).wait_send()
            if dx > 0:
                hand_on(xbuf, x_send, x_recv, k, dx).wait_send()
                b_copy(k, dx).wait_send()

        @pl.when(seg < last)
        def _():
            z_copy(k).wait_send()

        @pl.when(seg == last)
        def _():
            for dx in range(chips):
                f_copy(k, dx).wait_send()
                if dx > 0:
                    hand_on(fbuf, f_send, f_recv, k, dx).wait_send()

    @pl.when(seg == last)
    def _():
        for s in range(segments - 1):
            l_copy(s).wait_send()

    for p in range(1, inner):
        e_copy(p).wait_send()


def per_device(
    inner, segments, tokens, embedding, in_proj, out_proj, norm_gain, fir_taps, modal_rate,
    modal_residue, fir_state, modal_state, final_gain, unembed,
):
    steps = tokens.shape[0] - 1
    seqs = tokens.shape[1]
    rows = steps * seqs
    vocab, width = embedding.shape
    pieces = max(1, width // 256)
    sub = width // pieces
    chips = inner // 2
    full = inner * width
    vocab_local = unembed.shape[1]
    padded = max(128, vocab_local)
    block = seqs // segments
    whole = pl.BlockSpec(memory_space=pltpu.VMEM)
    in_hbm = pl.BlockSpec(memory_space=pltpu.HBM)
    dma = pltpu.SemaphoreType.DMA
    fir_by_tap = jnp.transpose(fir_state, (0, 2, 1, 3))
    operands = (
        tokens, norm_gain, final_gain[None], jnp.transpose(fir_taps, (1, 0, 2)), modal_rate,
        modal_residue, embedding, in_proj, out_proj, fir_by_tap, modal_state, unembed,
    )
    packed, product = pl.pallas_call(
        functools.partial(kernel, pieces, inner, segments),
        out_shape=(
            jax.ShapeDtypeStruct((steps, block, padded + 128), F32),
            jax.ShapeDtypeStruct((steps, seqs, width), F32),
        ),
        in_specs=[in_hbm] * len(operands),
        out_specs=(whole, in_hbm),
        scratch_shapes=[
            pltpu.VMEM((steps, seqs, width), F32),
            *[pltpu.VMEM(o.shape, o.dtype) for o in operands[:6]],
            pltpu.VMEM((vocab, width), BF16),
            pltpu.VMEM((inner, 3, width, width), BF16),
            pltpu.VMEM((inner * pieces, width, sub), BF16),
            pltpu.VMEM(fir_by_tap.shape[1:], F32),
            pltpu.VMEM(modal_state.shape[1:], F32),
            pltpu.VMEM((full, vocab_local), BF16),
            pltpu.VMEM((inner * pieces, rows, sub), BF16),
            pltpu.VMEM((inner * pieces, rows, sub), BF16),
            pltpu.VMEM((pieces, chips, rows, sub), BF16),
            pltpu.VMEM((pieces, chips, rows, sub), BF16),
            pltpu.VMEM((chips * pieces, rows, sub), BF16),
            pltpu.VMEM((chips * pieces, rows, sub), BF16),
            pltpu.VMEM((pieces, rows, sub), BF16),
            pltpu.VMEM((3, rows, width), F32),
            pltpu.VMEM((chips, rows, sub), F32),
            pltpu.VMEM((rows, 128), F32),
            pltpu.VMEM((steps, seqs, width), F32),
            pltpu.VMEM((steps, 1, width), F32),
            pltpu.VMEM((rows, width), BF16),
            pltpu.VMEM((rows, padded), F32),
            pltpu.VMEM((segments, steps, block, padded), F32),
            pltpu.VMEM((steps, block, padded), F32),
            pltpu.VMEM((inner, steps, block, 128), F32),
            dma,
            dma((6,)),
            dma,
            dma((inner * 3,)),
            dma((inner * pieces,)),
            dma,
            dma,
            dma((inner * pieces,)),
            dma((inner * pieces,)),
            dma((pieces,)),
            dma((pieces,)),
            dma((chips * pieces,)),
            dma((chips * pieces,)),
            dma((pieces,)),
            dma((inner * pieces,)),
            dma((inner * pieces,)),
            dma((segments,)),
            dma,
            dma((inner,)),
            dma((inner,)),
        ],
        compiler_params=pltpu.CompilerParams(
            collective_id=0, has_side_effects=True, vmem_limit_bytes=60 * 1024 * 1024
        ),
    )(*operands)
    is_short = lax.axis_index("segment") % 2 == 0
    shifted = jnp.concatenate([fir_by_tap[0], product], axis=0)[steps:]
    fir_out = jnp.where(is_short, shifted, fir_by_tap[0])
    decay = jnp.exp(-modal_rate[0])[None]
    mode_values = modal_state[0]
    for t in range(steps):
        mode_values = decay * mode_values + (1.0 - decay) * product[t][:, None, :]
    modal_out = jnp.where(is_short, modal_state[0], mode_values)
    return (
        packed[..., :vocab_local],
        packed[..., padded],
        jnp.transpose(fir_out, (1, 0, 2))[None],
        modal_out[None],
    )


def solution(mesh):
    inner = mesh.shape["inner"]
    segments = mesh.shape["segment"]
    return jax.shard_map(
        functools.partial(per_device, inner, segments),
        mesh=mesh,
        in_specs=(
            P(None, "groups"),
            P(None, "inner"),
            P("segment", None, None, "inner"),
            P("segment", "inner", None),
            P("segment", None),
            P("segment", None, "inner"),
            P("segment", None, "inner"),
            P("segment", None, "inner"),
            P("segment", "groups", None, "inner"),
            P("segment", "groups", None, "inner"),
            P(),
            P(None, "inner"),
        ),
        out_specs=(
            P(None, ("groups", "segment"), "inner"),
            P(None, ("groups", "segment")),
            P("segment", "groups", None, "inner"),
            P("segment", "groups", None, "inner"),
        ),
        check_vma=False,
    )
```

```python
import functools

import jax
import jax.numpy as jnp
from jax import lax
from jax.experimental import pallas as pl
from jax.experimental.pallas import tpu as pltpu
from jax.sharding import PartitionSpec as P

EPS = 1e-05
MESH = pl.DeviceIdType.MESH
F32 = jnp.float32
BF16 = jnp.bfloat16


def column_of(row, first, count):
    length = row.shape[1]
    down = lax.broadcasted_iota(jnp.int32, (count, length), 0) + first
    across = lax.broadcasted_iota(jnp.int32, (count, length), 1)
    picked = jnp.where(down == across, jnp.broadcast_to(row, (count, length)), 0.0)
    return jnp.sum(picked, axis=1, keepdims=True)


def kernel(
    pieces, inner, segments,
    tokens_h, norm_gain_h, final_gain_h, taps_h, rate_h, residue_h,
    embedding, w_in, w_out, fir_state, modal_state, unembed,
    packed_out, fir_new, modal_new,
    product_v, tokens, norm_gain, final_gain, taps, rate, residue,
    emb_v, in_v, out_v, fir_v, modal_v, unembed_v,
    xbuf, fbuf, abuf, arbuf, bbuf, brbuf, zbuf, acc, mixed, squares, state_part, coefs, gated,
    head_acc, scatter, lbuf, ebuf,
    out_state_sem, small_sem, emb_sem, in_sem, out_sem, state_sem, unembed_sem,
    x_send, x_recv, a_send, a_recv, b_send, b_recv, z_send, f_send, f_recv,
    l_send, l_recv, e_send, e_recv,
):
    seg = lax.axis_index("segment")
    me = lax.axis_index("inner")
    last = segments - 1
    chips = inner // 2
    chip = me // 2
    core = me % 2
    steps = tokens.shape[0] - 1
    seqs = tokens.shape[1]
    rows = steps * seqs
    width = emb_v.shape[1]
    sub = width // pieces
    vocab = emb_v.shape[0]
    vocab_local = unembed.shape[1]
    padded = lbuf.shape[2]
    block = seqs // segments
    depth = fir_v.shape[0]
    full = inner * width
    is_short = seg % 2 == 0
    sibling = chip * 2 + (core + 1) % 2

    def member(dx, dc):
        return (chip + dx) % chips * 2 + (core + dc) % 2

    def remote(src, dst, send, recv, where):
        return pltpu.make_async_remote_copy(
            src_ref=src, dst_ref=dst, send_sem=send, recv_sem=recv,
            device_id=where, device_id_type=MESH,
        )

    def arrival(ref, sem):
        pltpu.make_async_copy(ref, ref, sem).wait()

    barrier = pltpu.get_barrier_semaphore()
    for p in range(1, inner):
        pl.semaphore_signal(
            barrier, inc=1, device_id={"inner": member(p // 2, p % 2)}, device_id_type=MESH
        )
    for d in range(1, segments):
        pl.semaphore_signal(
            barrier, inc=1, device_id={"segment": (seg + d) % segments}, device_id_type=MESH
        )

    emb_copy = pltpu.make_async_copy(embedding, emb_v, emb_sem)
    fir_copy = pltpu.make_async_copy(fir_state.at[0], fir_v, state_sem)
    modal_copy = pltpu.make_async_copy(modal_state.at[0], modal_v, state_sem)
    unembed_copy = pltpu.make_async_copy(unembed, unembed_v, unembed_sem)
    small = [
        pltpu.make_async_copy(source, target, small_sem.at[index])
        for index, (source, target) in enumerate((
            (tokens_h, tokens), (taps_h, taps), (rate_h, rate), (residue_h, residue),
            (norm_gain_h, norm_gain), (final_gain_h, final_gain),
        ))
    ]

    def in_copy(q, j):
        return pltpu.make_async_copy(
            w_in.at[0, j, pl.ds(pl.multiple_of(q * width, width), width), :],
            in_v.at[q, j],
            in_sem.at[q * 3 + j],
        )

    def out_copy(q, k):
        return pltpu.make_async_copy(
            w_out.at[0, :, pl.ds(pl.multiple_of(q * width + k * sub, sub), sub)],
            out_v.at[q * pieces + k],
            out_sem.at[q * pieces + k],
        )

    small[0].start()

    @pl.when(seg == 0)
    def _():
        emb_copy.start()

    for copy in small[1:]:
        copy.start()

    @pl.when(is_short)
    def _():
        fir_copy.start()

    @pl.when(jnp.logical_not(is_short))
    def _():
        modal_copy.start()

    for dx, dc in (
        [(0, 0), (0, 1)] + [(dx, 0) for dx in range(1, chips)] + [(dx, 1) for dx in range(1, chips)]
    ):
        for j in range(3):
            in_copy(member(dx, dc), j).start()

    @pl.loop(0, pieces * inner)
    def _(t):
        out_copy(member(t % chips, (t // chips + 1) % 2), t // inner).start()

    unembed_copy.start()

    fir_whole = pltpu.make_async_copy(fir_state.at[0], fir_new, out_state_sem.at[0])
    fir_shift = pltpu.make_async_copy(
        fir_state.at[0, pl.ds(steps, depth - steps)],
        fir_new.at[pl.ds(0, depth - steps)],
        out_state_sem.at[0],
    )
    fir_latest = pltpu.make_async_copy(
        product_v, fir_new.at[pl.ds(depth - steps, steps)], out_state_sem.at[1]
    )
    modal_whole = pltpu.make_async_copy(modal_state.at[0], modal_new, out_state_sem.at[2])
    modal_done = pltpu.make_async_copy(modal_v, modal_new, out_state_sem.at[2])

    @pl.when(is_short)
    def _():
        fir_shift.start()
        modal_whole.start()

    @pl.when(jnp.logical_not(is_short))
    def _():
        fir_whole.start()

    small[0].wait()

    def gather_copy(buf, source, send, recv, k, dx):
        where = sibling if dx == 0 else member(dx, 0)
        return remote(
            source, buf.at[me * pieces + k], send.at[dx * pieces + k],
            recv.at[me * pieces + k], {"inner": where},
        )

    def hand_on(buf, send, recv, k, dx):
        q = member(dx, 0)
        return remote(
            buf.at[q * pieces + k], buf.at[q * pieces + k],
            send.at[(chips + dx) * pieces + k], recv.at[q * pieces + k], {"inner": sibling},
        )

    def x_copy(k, dx):
        return gather_copy(xbuf, xbuf.at[me * pieces + k], x_send, x_recv, k, dx)

    def f_copy(k, dx):
        return gather_copy(fbuf, zbuf.at[k], f_send, f_recv, k, dx)

    def spread(copy_of, k):
        for dx in range(chips - 1, -1, -1):
            copy_of(k, dx).start()

    def pass_on(buf, send, recv):
        for k in range(pieces):
            for dx in range(1, chips):
                q = member(dx, 0)
                arrival(buf.at[q * pieces + k], recv.at[q * pieces + k])
                hand_on(buf, send, recv, k, dx).start()

    @pl.when(seg == 0)
    def _():
        ids = jnp.concatenate(
            [column_of(tokens[pl.ds(t, 1), :].astype(F32), 0, seqs) for t in range(steps)], axis=0
        ).astype(jnp.int32)
        hot = lax.broadcasted_iota(jnp.int32, (rows, vocab), 1) == ids
        hot = hot.astype(F32).astype(BF16)
        emb_copy.wait()
        for k in range(pieces):
            looked_up = jnp.dot(
                hot, emb_v[:, k * sub:(k + 1) * sub], preferred_element_type=F32
            )
            xbuf[me * pieces + k] = looked_up.astype(BF16)

    pl.semaphore_wait(barrier, inner - 1 + segments - 1)

    @pl.when(seg == 0)
    def _():
        for k in range(pieces):
            spread(x_copy, k)

    for copy in small[1:]:
        copy.wait()

    acc[...] = jnp.zeros_like(acc)
    squares[...] = jnp.zeros_like(squares)

    @pl.when(is_short)
    def _():
        fir_copy.wait()
        for t in range(steps):
            coefs[t] = taps[t] if t <= depth else jnp.zeros((1, width), F32)
            for c in range(0, width, 256):
                cols = slice(c, c + 256)
                total = jnp.zeros((seqs, 256), F32)
                for i in range(depth - t):
                    total = total + fir_v[i + t, :, cols] * taps[depth - i, :, cols]
                state_part[t, :, cols] = total

    @pl.when(jnp.logical_not(is_short))
    def _():
        decay = jnp.exp(-rate[0])
        weight = residue[0] * (1.0 - decay)
        for t in range(steps):
            coef = jnp.sum(weight, axis=0, keepdims=True)
            coefs[t] = coef + taps[0] if t == 0 else coef
            weight = weight * decay
        modal_copy.wait()

        @pl.loop(0, seqs)
        def _(b):
            value = modal_v[b]
            for t in range(steps):
                value = value * decay
                state_part[t, pl.ds(b, 1), :] = jnp.sum(value * residue[0], axis=0, keepdims=True)

    def take(values, gain):
        values = values.astype(F32)
        total = squares[...]
        for c in range(0, values.shape[1], 128):
            piece = values[:, c:c + 128]
            total = total + piece * piece
        squares[...] = total
        return (values * gain).astype(BF16)

    def block_of(buf, q):
        return jnp.concatenate([buf[q * pieces + k] for k in range(pieces)], axis=1)

    @pl.loop(0, pieces)
    def _(k):
        @pl.when(seg > 0)
        def _():
            arrival(xbuf.at[me * pieces + k], x_recv.at[me * pieces + k])
            spread(x_copy, k)

        @pl.when(k == 0)
        def _():
            for j in range(3):
                in_copy(me, j).wait()

        offset = pl.multiple_of(me * width + k * sub, sub)
        scaled = take(xbuf[me * pieces + k], norm_gain[:, pl.ds(offset, sub)])
        depth_rows = pl.ds(pl.multiple_of(k * sub, sub), sub)
        for j in range(3):
            acc[j] += jnp.dot(scaled, in_v[me, j, depth_rows, :], preferred_element_type=F32)

    @pl.loop(1, inner)
    def _(t):
        q = member(jnp.where(t == 1, 0, jnp.where(t <= chips, t - 1, t - chips)),
                   jnp.where((t == 1) | (t > chips), 1, 0))

        @pl.when(t == 2)
        def _():
            pass_on(xbuf, x_send, x_recv)

        @pl.when((t == 1) | (t > chips))
        def _():
            for k in range(pieces):
                arrival(xbuf.at[q * pieces + k], x_recv.at[q * pieces + k])

        offset = pl.multiple_of(q * width, width)
        scaled = take(block_of(xbuf, q), norm_gain[:, pl.ds(offset, width)])
        for j in range(3):
            in_copy(q, j).wait()
            acc[j] += jnp.dot(scaled, in_v[q, j], preferred_element_type=F32)

    scale = lax.rsqrt(jnp.sum(squares[...], axis=1, keepdims=True) / full + EPS)
    for c in range(0, width, sub):
        cols = slice(c, c + sub)
        products = []
        for t in range(steps):
            part = slice(t * seqs, (t + 1) * seqs)
            scale_t = scale[part]
            product = (acc[1, part, cols] * scale_t) * (acc[2, part, cols] * scale_t)
            products.append(product)
            product_v[t, :, cols] = product
            filtered = state_part[t, :, cols]
            for u in range(t + 1):
                filtered = filtered + coefs[t - u, :, cols] * products[u]
            gated[part, cols] = (acc[0, part, cols] * scale_t * filtered).astype(BF16)

    @pl.when(is_short)
    def _():
        fir_latest.start()

    def a_copy(k):
        return remote(abuf.at[k], arbuf.at[k], a_send.at[k], a_recv.at[k], {"inner": sibling})

    def b_copy(k, dx):
        return remote(
            bbuf.at[dx * pieces + k], brbuf.at[chip * pieces + k], b_send.at[dx * pieces + k],
            b_recv.at[chip * pieces + k], {"inner": member(dx, 0)},
        )

    def z_copy(k):
        return remote(
            zbuf.at[k], xbuf.at[me * pieces + k], z_send.at[k],
            x_recv.at[me * pieces + k], {"segment": (seg + 1) % segments},
        )

    def mix(q, k):
        out_copy(q, k).wait()
        return jnp.dot(gated[...], out_v[q * pieces + k], preferred_element_type=F32)

    for step in range(pieces + 2):
        k = step
        if k < pieces:
            for x in range(chips):
                abuf[k, x] = mix(x * 2 + (core + 1) % 2, k).astype(BF16)
            a_copy(k).start()
        k = step - 1
        if 0 <= k < pieces:
            arrival(arbuf.at[k], a_recv.at[k])
            for dx in range(chips - 1, 0, -1):
                total = mixed[k, dx] + arbuf[k, (chip + dx) % chips].astype(F32)
                bbuf[dx * pieces + k] = total.astype(BF16)
                b_copy(k, dx).start()
            total = mixed[k, 0] + arbuf[k, chip].astype(F32)
            mixed[k, 0] = total + xbuf[me * pieces + k].astype(F32)
        k = step
        if k < pieces:
            for dx in range(chips - 1, -1, -1):
                mixed[k, dx] = mix(member(dx, 0), k)
        k = step - 2
        if 0 <= k < pieces:
            total = mixed[k, 0]
            for dx in range(1, chips):
                source = (chip + dx) % chips * pieces + k
                arrival(brbuf.at[source], b_recv.at[source])
                total = total + brbuf[source].astype(F32)
            zbuf[k] = total.astype(BF16)

            @pl.when(seg < last)
            def _():
                z_copy(k).start()

            @pl.when(seg == last)
            def _():
                spread(f_copy, k)

    @pl.when(jnp.logical_not(is_short))
    def _():
        decay = jnp.exp(-rate[0])

        @pl.loop(0, seqs)
        def _(b):
            value = modal_v[b]
            for t in range(steps):
                value = decay * value + (1.0 - decay) * product_v[t, pl.ds(b, 1), :]
            modal_v[b] = value

        modal_done.start()

    unembed_copy.wait()

    def l_copy(s):
        return remote(scatter.at[s], lbuf, l_send.at[s], l_recv, {"segment": s})

    @pl.when(seg == last)
    def _():
        squares[...] = jnp.zeros_like(squares)
        head_acc[...] = jnp.zeros_like(head_acc)

        def head(values, q):
            offset = pl.multiple_of(q * width, width)
            scaled = take(values, final_gain[:, pl.ds(offset, width)])
            head_acc[:, :vocab_local] += jnp.dot(
                scaled, unembed_v[pl.ds(offset, width), :], preferred_element_type=F32
            )

        head(jnp.concatenate([zbuf[k] for k in range(pieces)], axis=1), me)
        pass_on(fbuf, f_send, f_recv)

        @pl.loop(1, inner)
        def _(t):
            q = member(t % chips, t // chips)

            @pl.when(t >= chips)
            def _():
                for k in range(pieces):
                    arrival(fbuf.at[q * pieces + k], f_recv.at[q * pieces + k])

            head(block_of(fbuf, q), q)

        final_scale = lax.rsqrt(jnp.sum(squares[...], axis=1, keepdims=True) / full + EPS)
        logits = head_acc[...] * final_scale
        for s in range(segments):
            for t in range(steps):
                start = t * seqs + s * block
                if s < last:
                    scatter[s, t] = logits[start:start + block]
                else:
                    lbuf[t] = logits[start:start + block]
            if s < last:
                l_copy(s).start()

    @pl.when(seg < last)
    def _():
        arrival(lbuf, l_recv)

    def e_copy(p):
        return remote(
            ebuf.at[me], ebuf.at[me], e_send.at[p], e_recv.at[me],
            {"inner": member(p // 2, p % 2)},
        )

    columns = lax.broadcasted_iota(jnp.int32, (block, vocab_local), 1) + me * vocab_local
    lanes = lax.broadcasted_iota(jnp.int32, (block, 128), 1)
    for t in range(steps):
        logits_t = lbuf[t, :, :vocab_local]
        packed_out[t, :, :vocab_local] = logits_t
        target = column_of(tokens[pl.ds(t + 1, 1), :].astype(F32), seg * block, block)
        hit = columns == target.astype(jnp.int32)
        exp_sum = jnp.sum(jnp.exp(logits_t), axis=1, keepdims=True)
        target_part = jnp.sum(jnp.where(hit, logits_t, 0.0), axis=1, keepdims=True)
        ebuf[me, t] = jnp.where(lanes == 0, exp_sum, target_part)
    for p in range(inner - 1, 0, -1):
        e_copy(p).start()
    sums = ebuf[me]
    for p in range(1, inner):
        q = member(p // 2, p % 2)
        arrival(ebuf.at[q], e_recv.at[q])
        sums = sums + ebuf[q]
    for t in range(steps):
        logprob = sums[t, :, 1:2] - jnp.log(sums[t, :, 0:1])
        packed_out[t, :, padded:] = jnp.broadcast_to(logprob, (block, 128))

    @pl.when(is_short)
    def _():
        fir_shift.wait()
        fir_latest.wait()
        modal_whole.wait()

    @pl.when(jnp.logical_not(is_short))
    def _():
        fir_whole.wait()
        modal_done.wait()

    @pl.loop(0, pieces)
    def _(k):
        a_copy(k).wait_send()
        for dx in range(chips):
            x_copy(k, dx).wait_send()
            if dx > 0:
                hand_on(xbuf, x_send, x_recv, k, dx).wait_send()
                b_copy(k, dx).wait_send()

        @pl.when(seg < last)
        def _():
            z_copy(k).wait_send()

        @pl.when(seg == last)
        def _():
            for dx in range(chips):
                f_copy(k, dx).wait_send()
                if dx > 0:
                    hand_on(fbuf, f_send, f_recv, k, dx).wait_send()

    @pl.when(seg == last)
    def _():
        for s in range(segments - 1):
            l_copy(s).wait_send()

    for p in range(1, inner):
        e_copy(p).wait_send()


def hand_out(vocab_local, padded, packed, fir_new, modal_new, logits, logprob, fir, modal, sems):
    copies = [
        pltpu.make_async_copy(fir_new, fir.at[0], sems.at[0]),
        pltpu.make_async_copy(modal_new, modal.at[0], sems.at[1]),
    ]
    for copy in copies:
        copy.start()
    steps, block = logprob.shape
    down = lax.broadcasted_iota(jnp.int32, (block, block), 0)
    across = lax.broadcasted_iota(jnp.int32, (block, block), 1)
    for t in range(steps):
        logits[t] = packed[t, :, :vocab_local]
        spread_out = packed[t, :, padded:padded + block]
        logprob[t:t + 1, :] = jnp.sum(
            jnp.where(down == across, spread_out, 0.0), axis=0, keepdims=True
        )
    for copy in copies:
        copy.wait()


def per_device(
    inner, segments, tokens, embedding, in_proj, out_proj, norm_gain, fir_taps, modal_rate,
    modal_residue, fir_state, modal_state, final_gain, unembed,
):
    steps = tokens.shape[0] - 1
    seqs = tokens.shape[1]
    rows = steps * seqs
    vocab, width = embedding.shape
    pieces = max(1, width // 256)
    sub = width // pieces
    chips = inner // 2
    full = inner * width
    vocab_local = unembed.shape[1]
    padded = max(128, vocab_local)
    block = seqs // segments
    whole = pl.BlockSpec(memory_space=pltpu.VMEM)
    in_hbm = pl.BlockSpec(memory_space=pltpu.HBM)
    dma = pltpu.SemaphoreType.DMA
    fir_by_tap = jnp.transpose(fir_state, (0, 2, 1, 3))
    operands = (
        tokens, norm_gain, final_gain[None], jnp.transpose(fir_taps, (1, 0, 2)), modal_rate,
        modal_residue, embedding, in_proj, out_proj, fir_by_tap, modal_state, unembed,
    )
    packed, fir_new, modal_new = pl.pallas_call(
        functools.partial(kernel, pieces, inner, segments),
        out_shape=(
            jax.ShapeDtypeStruct((steps, block, padded + 128), F32),
            jax.ShapeDtypeStruct(fir_by_tap.shape[1:], F32),
            jax.ShapeDtypeStruct(modal_state.shape[1:], F32),
        ),
        in_specs=[in_hbm] * len(operands),
        out_specs=(whole, in_hbm, in_hbm),
        scratch_shapes=[
            pltpu.VMEM((steps, seqs, width), F32),
            *[pltpu.VMEM(o.shape, o.dtype) for o in operands[:6]],
            pltpu.VMEM((vocab, width), BF16),
            pltpu.VMEM((inner, 3, width, width), BF16),
            pltpu.VMEM((inner * pieces, width, sub), BF16),
            pltpu.VMEM(fir_by_tap.shape[1:], F32),
            pltpu.VMEM(modal_state.shape[1:], F32),
            pltpu.VMEM((full, vocab_local), BF16),
            pltpu.VMEM((inner * pieces, rows, sub), BF16),
            pltpu.VMEM((inner * pieces, rows, sub), BF16),
            pltpu.VMEM((pieces, chips, rows, sub), BF16),
            pltpu.VMEM((pieces, chips, rows, sub), BF16),
            pltpu.VMEM((chips * pieces, rows, sub), BF16),
            pltpu.VMEM((chips * pieces, rows, sub), BF16),
            pltpu.VMEM((pieces, rows, sub), BF16),
            pltpu.VMEM((3, rows, width), F32),
            pltpu.VMEM((pieces, chips, rows, sub), F32),
            pltpu.VMEM((rows, 128), F32),
            pltpu.VMEM((steps, seqs, width), F32),
            pltpu.VMEM((steps, 1, width), F32),
            pltpu.VMEM((rows, width), BF16),
            pltpu.VMEM((rows, padded), F32),
            pltpu.VMEM((segments, steps, block, padded), F32),
            pltpu.VMEM((steps, block, padded), F32),
            pltpu.VMEM((inner, steps, block, 128), F32),
            dma((3,)),
            dma((6,)),
            dma,
            dma((inner * 3,)),
            dma((inner * pieces,)),
            dma,
            dma,
            dma((inner * pieces,)),
            dma((inner * pieces,)),
            dma((pieces,)),
            dma((pieces,)),
            dma((chips * pieces,)),
            dma((chips * pieces,)),
            dma((pieces,)),
            dma((inner * pieces,)),
            dma((inner * pieces,)),
            dma((segments,)),
            dma,
            dma((inner,)),
            dma((inner,)),
        ],
        compiler_params=pltpu.CompilerParams(
            collective_id=0, has_side_effects=True, vmem_limit_bytes=60 * 1024 * 1024
        ),
    )(*operands)
    logits, logprob, fir_out, modal_out = pl.pallas_call(
        functools.partial(hand_out, vocab_local, padded),
        out_shape=(
            jax.ShapeDtypeStruct((steps, block, vocab_local), F32),
            jax.ShapeDtypeStruct((steps, block), F32),
            jax.ShapeDtypeStruct(fir_by_tap.shape, F32),
            jax.ShapeDtypeStruct(modal_state.shape, F32),
        ),
        in_specs=[whole, in_hbm, in_hbm],
        out_specs=(whole, whole, in_hbm, in_hbm),
        scratch_shapes=[dma((2,))],
        compiler_params=pltpu.CompilerParams(vmem_limit_bytes=60 * 1024 * 1024),
    )(packed, fir_new, modal_new)
    return (logits, logprob, jnp.transpose(fir_out, (0, 2, 1, 3)), modal_out)


def solution(mesh):
    inner = mesh.shape["inner"]
    segments = mesh.shape["segment"]
    return jax.shard_map(
        functools.partial(per_device, inner, segments),
        mesh=mesh,
        in_specs=(
            P(None, "groups"),
            P(None, "inner"),
            P("segment", None, None, "inner"),
            P("segment", "inner", None),
            P("segment", None),
            P("segment", None, "inner"),
            P("segment", None, "inner"),
            P("segment", None, "inner"),
            P("segment", "groups", None, "inner"),
            P("segment", "groups", None, "inner"),
            P(),
            P(None, "inner"),
        ),
        out_specs=(
            P(None, ("groups", "segment"), "inner"),
            P(None, ("groups", "segment")),
            P("segment", "groups", None, "inner"),
            P("segment", "groups", None, "inner"),
        ),
        check_vma=False,
    )
```

```python
import functools

import jax
import jax.numpy as jnp
from jax import lax
from jax.experimental import pallas as pl
from jax.experimental.pallas import tpu as pltpu
from jax.sharding import PartitionSpec as P

EPS = 1e-05
MESH = pl.DeviceIdType.MESH
F32 = jnp.float32
BF16 = jnp.bfloat16


def column_of(row, first, count):
    length = row.shape[1]
    down = lax.broadcasted_iota(jnp.int32, (count, length), 0) + first
    across = lax.broadcasted_iota(jnp.int32, (count, length), 1)
    picked = jnp.where(down == across, jnp.broadcast_to(row, (count, length)), 0.0)
    return jnp.sum(picked, axis=1, keepdims=True)


def kernel(
    pieces, inner, segments,
    tokens_h, norm_gain_h, final_gain_h, taps_h, rate_h, residue_h,
    embedding, w_in, w_out, fir_state, modal_state, unembed,
    packed_out, fir_new, modal_new,
    product_v, tokens, norm_gain, final_gain, taps, rate, residue,
    emb_v, in_v, out_v, fir_v, modal_v, unembed_v,
    xbuf, fbuf, abuf, arbuf, bbuf, brbuf, zbuf, acc, mixed, squares, state_part, coefs, gated,
    head_acc, scatter, lbuf, ebuf,
    out_state_sem, small_sem, emb_sem, in_sem, out_sem, state_sem, unembed_sem,
    x_send, x_recv, a_send, a_recv, b_send, b_recv, z_send, f_send, f_recv,
    l_send, l_recv, e_send, e_recv,
):
    seg = lax.axis_index("segment")
    me = lax.axis_index("inner")
    last = segments - 1
    chips = inner // 2
    chip = me // 2
    core = me % 2
    steps = tokens.shape[0] - 1
    seqs = tokens.shape[1]
    rows = steps * seqs
    width = emb_v.shape[1]
    sub = width // pieces
    vocab = emb_v.shape[0]
    vocab_local = unembed.shape[1]
    padded = lbuf.shape[2]
    block = seqs // segments
    depth = fir_v.shape[0]
    full = inner * width
    is_short = seg % 2 == 0
    sibling = chip * 2 + (core + 1) % 2

    def member(dx, dc):
        return (chip + dx) % chips * 2 + (core + dc) % 2

    def remote(src, dst, send, recv, where):
        return pltpu.make_async_remote_copy(
            src_ref=src, dst_ref=dst, send_sem=send, recv_sem=recv,
            device_id=where, device_id_type=MESH,
        )

    def arrival(ref, sem):
        pltpu.make_async_copy(ref, ref, sem).wait()

    barrier = pltpu.get_barrier_semaphore()
    for p in range(1, inner):
        pl.semaphore_signal(
            barrier, inc=1, device_id={"inner": member(p // 2, p % 2)}, device_id_type=MESH
        )
    for d in range(1, segments):
        pl.semaphore_signal(
            barrier, inc=1, device_id={"segment": (seg + d) % segments}, device_id_type=MESH
        )

    emb_copy = pltpu.make_async_copy(embedding, emb_v, emb_sem)
    fir_copy = pltpu.make_async_copy(fir_state.at[0], fir_v, state_sem.at[0])
    modal_copy = pltpu.make_async_copy(modal_state.at[0], modal_v, state_sem.at[1])
    unembed_copy = pltpu.make_async_copy(unembed, unembed_v, unembed_sem)
    small = [
        pltpu.make_async_copy(source, target, small_sem.at[index])
        for index, (source, target) in enumerate((
            (tokens_h, tokens), (taps_h, taps), (rate_h, rate), (residue_h, residue),
            (norm_gain_h, norm_gain), (final_gain_h, final_gain),
        ))
    ]

    def in_copy(q, j):
        return pltpu.make_async_copy(
            w_in.at[0, j, pl.ds(pl.multiple_of(q * width, width), width), :],
            in_v.at[q, j],
            in_sem.at[q * 3 + j],
        )

    def out_copy(q, k):
        return pltpu.make_async_copy(
            w_out.at[0, :, pl.ds(pl.multiple_of(q * width + k * sub, sub), sub)],
            out_v.at[q * pieces + k],
            out_sem.at[q * pieces + k],
        )

    small[0].start()

    @pl.when(seg == 0)
    def _():
        emb_copy.start()

    for copy in small[1:]:
        copy.start()

    @pl.when(is_short)
    def _():
        fir_copy.start()

    @pl.when(jnp.logical_not(is_short))
    def _():
        modal_copy.start()

    for dx, dc in (
        [(0, 0), (0, 1)] + [(dx, 0) for dx in range(1, chips)] + [(dx, 1) for dx in range(1, chips)]
    ):
        for j in range(3):
            in_copy(member(dx, dc), j).start()

    @pl.loop(0, pieces * inner)
    def _(t):
        out_copy(member(t % chips, (t // chips + 1) % 2), t // inner).start()

    unembed_copy.start()

    @pl.when(is_short)
    def _():
        modal_copy.start()

    @pl.when(jnp.logical_not(is_short))
    def _():
        fir_copy.start()

    fir_whole = pltpu.make_async_copy(fir_v, fir_new, out_state_sem.at[0])
    fir_shift = pltpu.make_async_copy(
        fir_v.at[pl.ds(steps, depth - steps)],
        fir_new.at[pl.ds(0, depth - steps)],
        out_state_sem.at[0],
    )
    fir_latest = pltpu.make_async_copy(
        product_v, fir_new.at[pl.ds(depth - steps, steps)], out_state_sem.at[1]
    )
    modal_done = pltpu.make_async_copy(modal_v, modal_new, out_state_sem.at[2])

    small[0].wait()

    def gather_copy(buf, source, send, recv, k, dx):
        where = sibling if dx == 0 else member(dx, 0)
        return remote(
            source, buf.at[me * pieces + k], send.at[dx * pieces + k],
            recv.at[me * pieces + k], {"inner": where},
        )

    def hand_on(buf, send, recv, k, dx):
        q = member(dx, 0)
        return remote(
            buf.at[q * pieces + k], buf.at[q * pieces + k],
            send.at[(chips + dx) * pieces + k], recv.at[q * pieces + k], {"inner": sibling},
        )

    def x_copy(k, dx):
        return gather_copy(xbuf, xbuf.at[me * pieces + k], x_send, x_recv, k, dx)

    def f_copy(k, dx):
        return gather_copy(fbuf, zbuf.at[k], f_send, f_recv, k, dx)

    def spread(copy_of, k):
        for dx in range(chips - 1, -1, -1):
            copy_of(k, dx).start()

    def pass_on(buf, send, recv):
        for k in range(pieces):
            for dx in range(1, chips):
                q = member(dx, 0)
                arrival(buf.at[q * pieces + k], recv.at[q * pieces + k])
                hand_on(buf, send, recv, k, dx).start()

    @pl.when(seg == 0)
    def _():
        ids = jnp.concatenate(
            [column_of(tokens[pl.ds(t, 1), :].astype(F32), 0, seqs) for t in range(steps)], axis=0
        ).astype(jnp.int32)
        hot = lax.broadcasted_iota(jnp.int32, (rows, vocab), 1) == ids
        hot = hot.astype(F32).astype(BF16)
        emb_copy.wait()
        for k in range(pieces):
            looked_up = jnp.dot(
                hot, emb_v[:, k * sub:(k + 1) * sub], preferred_element_type=F32
            )
            xbuf[me * pieces + k] = looked_up.astype(BF16)

    pl.semaphore_wait(barrier, inner - 1 + segments - 1)

    @pl.when(seg == 0)
    def _():
        for k in range(pieces):
            spread(x_copy, k)

    for copy in small[1:]:
        copy.wait()

    acc[...] = jnp.zeros_like(acc)
    squares[...] = jnp.zeros_like(squares)

    @pl.when(is_short)
    def _():
        fir_copy.wait()
        for t in range(steps):
            coefs[t] = taps[t] if t <= depth else jnp.zeros((1, width), F32)
            for c in range(0, width, 256):
                cols = slice(c, c + 256)
                total = jnp.zeros((seqs, 256), F32)
                for i in range(depth - t):
                    total = total + fir_v[i + t, :, cols] * taps[depth - i, :, cols]
                state_part[t, :, cols] = total

    @pl.when(jnp.logical_not(is_short))
    def _():
        decay = jnp.exp(-rate[0])
        weight = residue[0] * (1.0 - decay)
        for t in range(steps):
            coef = jnp.sum(weight, axis=0, keepdims=True)
            coefs[t] = coef + taps[0] if t == 0 else coef
            weight = weight * decay
        modal_copy.wait()

        @pl.loop(0, seqs)
        def _(b):
            value = modal_v[b]
            for t in range(steps):
                value = value * decay
                state_part[t, pl.ds(b, 1), :] = jnp.sum(value * residue[0], axis=0, keepdims=True)

    def take(values, gain):
        values = values.astype(F32)
        total = squares[...]
        for c in range(0, values.shape[1], 128):
            piece = values[:, c:c + 128]
            total = total + piece * piece
        squares[...] = total
        return (values * gain).astype(BF16)

    def block_of(buf, q):
        return jnp.concatenate([buf[q * pieces + k] for k in range(pieces)], axis=1)

    @pl.loop(0, pieces)
    def _(k):
        @pl.when(seg > 0)
        def _():
            arrival(xbuf.at[me * pieces + k], x_recv.at[me * pieces + k])
            spread(x_copy, k)

        @pl.when(k == 0)
        def _():
            for j in range(3):
                in_copy(me, j).wait()

        offset = pl.multiple_of(me * width + k * sub, sub)
        scaled = take(xbuf[me * pieces + k], norm_gain[:, pl.ds(offset, sub)])
        depth_rows = pl.ds(pl.multiple_of(k * sub, sub), sub)
        for j in range(3):
            acc[j] += jnp.dot(scaled, in_v[me, j, depth_rows, :], preferred_element_type=F32)

    @pl.loop(1, inner)
    def _(t):
        q = member(jnp.where(t == 1, 0, jnp.where(t <= chips, t - 1, t - chips)),
                   jnp.where((t == 1) | (t > chips), 1, 0))

        @pl.when(t == 2)
        def _():
            pass_on(xbuf, x_send, x_recv)

        @pl.when((t == 1) | (t > chips))
        def _():
            for k in range(pieces):
                arrival(xbuf.at[q * pieces + k], x_recv.at[q * pieces + k])

        offset = pl.multiple_of(q * width, width)
        scaled = take(block_of(xbuf, q), norm_gain[:, pl.ds(offset, width)])
        for j in range(3):
            in_copy(q, j).wait()
            acc[j] += jnp.dot(scaled, in_v[q, j], preferred_element_type=F32)

    scale = lax.rsqrt(jnp.sum(squares[...], axis=1, keepdims=True) / full + EPS)
    for c in range(0, width, sub):
        cols = slice(c, c + sub)
        products = []
        for t in range(steps):
            part = slice(t * seqs, (t + 1) * seqs)
            scale_t = scale[part]
            product = (acc[1, part, cols] * scale_t) * (acc[2, part, cols] * scale_t)
            products.append(product)
            product_v[t, :, cols] = product
            filtered = state_part[t, :, cols]
            for u in range(t + 1):
                filtered = filtered + coefs[t - u, :, cols] * products[u]
            gated[part, cols] = (acc[0, part, cols] * scale_t * filtered).astype(BF16)

    @pl.when(is_short)
    def _():
        fir_shift.start()
        fir_latest.start()

    def a_copy(k):
        return remote(abuf.at[k], arbuf.at[k], a_send.at[k], a_recv.at[k], {"inner": sibling})

    def b_copy(k, dx):
        return remote(
            bbuf.at[dx * pieces + k], brbuf.at[chip * pieces + k], b_send.at[dx * pieces + k],
            b_recv.at[chip * pieces + k], {"inner": member(dx, 0)},
        )

    def z_copy(k):
        return remote(
            zbuf.at[k], xbuf.at[me * pieces + k], z_send.at[k],
            x_recv.at[me * pieces + k], {"segment": (seg + 1) % segments},
        )

    def mix(q, k):
        out_copy(q, k).wait()
        return jnp.dot(gated[...], out_v[q * pieces + k], preferred_element_type=F32)

    for step in range(pieces + 2):
        k = step
        if k < pieces:
            for x in range(chips):
                abuf[k, x] = mix(x * 2 + (core + 1) % 2, k).astype(BF16)
            a_copy(k).start()
        k = step - 1
        if 0 <= k < pieces:
            arrival(arbuf.at[k], a_recv.at[k])
            for dx in range(chips - 1, 0, -1):
                total = mixed[k, dx] + arbuf[k, (chip + dx) % chips].astype(F32)
                bbuf[dx * pieces + k] = total.astype(BF16)
                b_copy(k, dx).start()
            total = mixed[k, 0] + arbuf[k, chip].astype(F32)
            mixed[k, 0] = total + xbuf[me * pieces + k].astype(F32)
        k = step
        if k < pieces:
            for dx in range(chips - 1, -1, -1):
                mixed[k, dx] = mix(member(dx, 0), k)
        k = step - 2
        if 0 <= k < pieces:
            total = mixed[k, 0]
            for dx in range(1, chips):
                source = (chip + dx) % chips * pieces + k
                arrival(brbuf.at[source], b_recv.at[source])
                total = total + brbuf[source].astype(F32)
            zbuf[k] = total.astype(BF16)

            @pl.when(seg < last)
            def _():
                z_copy(k).start()

            @pl.when(seg == last)
            def _():
                spread(f_copy, k)

    @pl.when(is_short)
    def _():
        modal_copy.wait()

    @pl.when(jnp.logical_not(is_short))
    def _():
        fir_copy.wait()
        fir_whole.start()
        decay = jnp.exp(-rate[0])

        @pl.loop(0, seqs)
        def _(b):
            value = modal_v[b]
            for t in range(steps):
                value = decay * value + (1.0 - decay) * product_v[t, pl.ds(b, 1), :]
            modal_v[b] = value

    modal_done.start()

    unembed_copy.wait()

    def l_copy(s):
        return remote(scatter.at[s], lbuf, l_send.at[s], l_recv, {"segment": s})

    @pl.when(seg == last)
    def _():
        squares[...] = jnp.zeros_like(squares)
        head_acc[...] = jnp.zeros_like(head_acc)

        def head(values, q):
            offset = pl.multiple_of(q * width, width)
            scaled = take(values, final_gain[:, pl.ds(offset, width)])
            head_acc[:, :vocab_local] += jnp.dot(
                scaled, unembed_v[pl.ds(offset, width), :], preferred_element_type=F32
            )

        head(jnp.concatenate([zbuf[k] for k in range(pieces)], axis=1), me)
        pass_on(fbuf, f_send, f_recv)

        @pl.loop(1, inner)
        def _(t):
            q = member(t % chips, t // chips)

            @pl.when(t >= chips)
            def _():
                for k in range(pieces):
                    arrival(fbuf.at[q * pieces + k], f_recv.at[q * pieces + k])

            head(block_of(fbuf, q), q)

        final_scale = lax.rsqrt(jnp.sum(squares[...], axis=1, keepdims=True) / full + EPS)
        logits = head_acc[...] * final_scale
        for s in range(segments):
            for t in range(steps):
                start = t * seqs + s * block
                if s < last:
                    scatter[s, t] = logits[start:start + block]
                else:
                    lbuf[t] = logits[start:start + block]
            if s < last:
                l_copy(s).start()

    @pl.when(seg < last)
    def _():
        arrival(lbuf, l_recv)

    def e_copy(p):
        return remote(
            ebuf.at[me], ebuf.at[me], e_send.at[p], e_recv.at[me],
            {"inner": member(p // 2, p % 2)},
        )

    columns = lax.broadcasted_iota(jnp.int32, (block, vocab_local), 1) + me * vocab_local
    lanes = lax.broadcasted_iota(jnp.int32, (block, 128), 1)
    for t in range(steps):
        logits_t = lbuf[t, :, :vocab_local]
        packed_out[t, :, :vocab_local] = logits_t
        target = column_of(tokens[pl.ds(t + 1, 1), :].astype(F32), seg * block, block)
        hit = columns == target.astype(jnp.int32)
        exp_sum = jnp.sum(jnp.exp(logits_t), axis=1, keepdims=True)
        target_part = jnp.sum(jnp.where(hit, logits_t, 0.0), axis=1, keepdims=True)
        ebuf[me, t] = jnp.where(lanes == 0, exp_sum, target_part)
    for p in range(inner - 1, 0, -1):
        e_copy(p).start()
    sums = ebuf[me]
    for p in range(1, inner):
        q = member(p // 2, p % 2)
        arrival(ebuf.at[q], e_recv.at[q])
        sums = sums + ebuf[q]
    for t in range(steps):
        logprob = sums[t, :, 1:2] - jnp.log(sums[t, :, 0:1])
        packed_out[t, :, padded:] = jnp.broadcast_to(logprob, (block, 128))

    @pl.when(is_short)
    def _():
        fir_shift.wait()
        fir_latest.wait()

    @pl.when(jnp.logical_not(is_short))
    def _():
        fir_whole.wait()

    modal_done.wait()

    @pl.loop(0, pieces)
    def _(k):
        a_copy(k).wait_send()
        for dx in range(chips):
            x_copy(k, dx).wait_send()
            if dx > 0:
                hand_on(xbuf, x_send, x_recv, k, dx).wait_send()
                b_copy(k, dx).wait_send()

        @pl.when(seg < last)
        def _():
            z_copy(k).wait_send()

        @pl.when(seg == last)
        def _():
            for dx in range(chips):
                f_copy(k, dx).wait_send()
                if dx > 0:
                    hand_on(fbuf, f_send, f_recv, k, dx).wait_send()

    @pl.when(seg == last)
    def _():
        for s in range(segments - 1):
            l_copy(s).wait_send()

    for p in range(1, inner):
        e_copy(p).wait_send()


def hand_out(
    vocab_local, padded, packed, fir_new, modal_new, logits, logprob, fir, modal,
    fir_v, modal_v, in_sems, out_sems,
):
    parts = [(fir_new, fir_v, fir, i) for i in range(fir_v.shape[0])]
    share = modal_v.shape[0] // 4
    parts += [(modal_new, modal_v, modal, pl.ds(i * share, share)) for i in range(4)]
    arriving = [
        pltpu.make_async_copy(source.at[where], held.at[where], in_sems.at[i])
        for i, (source, held, _, where) in enumerate(parts)
    ]
    leaving = [
        pltpu.make_async_copy(held.at[where], target.at[0, where], out_sems.at[i])
        for i, (_, held, target, where) in enumerate(parts)
    ]
    for copy in arriving:
        copy.start()
    steps, block = logprob.shape
    down = lax.broadcasted_iota(jnp.int32, (block, block), 0)
    across = lax.broadcasted_iota(jnp.int32, (block, block), 1)
    for t in range(steps):
        logits[t] = packed[t, :, :vocab_local]
        spread_out = packed[t, :, padded:padded + block]
        logprob[t:t + 1, :] = jnp.sum(
            jnp.where(down == across, spread_out, 0.0), axis=0, keepdims=True
        )
    for before, after in zip(arriving, leaving):
        before.wait()
        after.start()
    for copy in leaving:
        copy.wait()


def per_device(
    inner, segments, tokens, embedding, in_proj, out_proj, norm_gain, fir_taps, modal_rate,
    modal_residue, fir_state, modal_state, final_gain, unembed,
):
    steps = tokens.shape[0] - 1
    seqs = tokens.shape[1]
    rows = steps * seqs
    vocab, width = embedding.shape
    pieces = max(1, width // 256)
    sub = width // pieces
    chips = inner // 2
    full = inner * width
    vocab_local = unembed.shape[1]
    padded = max(128, vocab_local)
    block = seqs // segments
    whole = pl.BlockSpec(memory_space=pltpu.VMEM)
    in_hbm = pl.BlockSpec(memory_space=pltpu.HBM)
    dma = pltpu.SemaphoreType.DMA
    fir_by_tap = jnp.transpose(fir_state, (0, 2, 1, 3))
    operands = (
        tokens, norm_gain, final_gain[None], jnp.transpose(fir_taps, (1, 0, 2)), modal_rate,
        modal_residue, embedding, in_proj, out_proj, fir_by_tap, modal_state, unembed,
    )
    packed, fir_new, modal_new = pl.pallas_call(
        functools.partial(kernel, pieces, inner, segments),
        out_shape=(
            jax.ShapeDtypeStruct((steps, block, padded + 128), F32),
            jax.ShapeDtypeStruct(fir_by_tap.shape[1:], F32),
            jax.ShapeDtypeStruct(modal_state.shape[1:], F32),
        ),
        in_specs=[in_hbm] * len(operands),
        out_specs=(whole, in_hbm, in_hbm),
        scratch_shapes=[
            pltpu.VMEM((steps, seqs, width), F32),
            *[pltpu.VMEM(o.shape, o.dtype) for o in operands[:6]],
            pltpu.VMEM((vocab, width), BF16),
            pltpu.VMEM((inner, 3, width, width), BF16),
            pltpu.VMEM((inner * pieces, width, sub), BF16),
            pltpu.VMEM(fir_by_tap.shape[1:], F32),
            pltpu.VMEM(modal_state.shape[1:], F32),
            pltpu.VMEM((full, vocab_local), BF16),
            pltpu.VMEM((inner * pieces, rows, sub), BF16),
            pltpu.VMEM((inner * pieces, rows, sub), BF16),
            pltpu.VMEM((pieces, chips, rows, sub), BF16),
            pltpu.VMEM((pieces, chips, rows, sub), BF16),
            pltpu.VMEM((chips * pieces, rows, sub), BF16),
            pltpu.VMEM((chips * pieces, rows, sub), BF16),
            pltpu.VMEM((pieces, rows, sub), BF16),
            pltpu.VMEM((3, rows, width), F32),
            pltpu.VMEM((pieces, chips, rows, sub), F32),
            pltpu.VMEM((rows, 128), F32),
            pltpu.VMEM((steps, seqs, width), F32),
            pltpu.VMEM((steps, 1, width), F32),
            pltpu.VMEM((rows, width), BF16),
            pltpu.VMEM((rows, padded), F32),
            pltpu.VMEM((segments, steps, block, padded), F32),
            pltpu.VMEM((steps, block, padded), F32),
            pltpu.VMEM((inner, steps, block, 128), F32),
            dma((3,)),
            dma((6,)),
            dma,
            dma((inner * 3,)),
            dma((inner * pieces,)),
            dma((2,)),
            dma,
            dma((inner * pieces,)),
            dma((inner * pieces,)),
            dma((pieces,)),
            dma((pieces,)),
            dma((chips * pieces,)),
            dma((chips * pieces,)),
            dma((pieces,)),
            dma((inner * pieces,)),
            dma((inner * pieces,)),
            dma((segments,)),
            dma,
            dma((inner,)),
            dma((inner,)),
        ],
        compiler_params=pltpu.CompilerParams(
            collective_id=0, has_side_effects=True, vmem_limit_bytes=60 * 1024 * 1024
        ),
    )(*operands)
    logits, logprob, fir_out, modal_out = pl.pallas_call(
        functools.partial(hand_out, vocab_local, padded),
        out_shape=(
            jax.ShapeDtypeStruct((steps, block, vocab_local), F32),
            jax.ShapeDtypeStruct((steps, block), F32),
            jax.ShapeDtypeStruct(fir_by_tap.shape, F32),
            jax.ShapeDtypeStruct(modal_state.shape, F32),
        ),
        in_specs=[whole, in_hbm, in_hbm],
        out_specs=(whole, whole, in_hbm, in_hbm),
        scratch_shapes=[
            pltpu.VMEM(fir_new.shape, F32),
            pltpu.VMEM(modal_new.shape, F32),
            dma((fir_new.shape[0] + 4,)),
            dma((fir_new.shape[0] + 4,)),
        ],
        compiler_params=pltpu.CompilerParams(vmem_limit_bytes=60 * 1024 * 1024),
    )(packed, fir_new, modal_new)
    return (logits, logprob, jnp.transpose(fir_out, (0, 2, 1, 3)), modal_out)


def solution(mesh):
    inner = mesh.shape["inner"]
    segments = mesh.shape["segment"]
    return jax.shard_map(
        functools.partial(per_device, inner, segments),
        mesh=mesh,
        in_specs=(
            P(None, "groups"),
            P(None, "inner"),
            P("segment", None, None, "inner"),
            P("segment", "inner", None),
            P("segment", None),
            P("segment", None, "inner"),
            P("segment", None, "inner"),
            P("segment", None, "inner"),
            P("segment", "groups", None, "inner"),
            P("segment", "groups", None, "inner"),
            P(),
            P(None, "inner"),
        ),
        out_specs=(
            P(None, ("groups", "segment"), "inner"),
            P(None, ("groups", "segment")),
            P("segment", "groups", None, "inner"),
            P("segment", "groups", None, "inner"),
        ),
        check_vma=False,
    )
```

```python
import functools

import jax
import jax.numpy as jnp
from jax import lax
from jax.experimental import pallas as pl
from jax.experimental.pallas import tpu as pltpu
from jax.sharding import PartitionSpec as P

EPS = 1e-05
MESH = pl.DeviceIdType.MESH
F32 = jnp.float32
BF16 = jnp.bfloat16


def column_of(row, first, count):
    length = row.shape[1]
    down = lax.broadcasted_iota(jnp.int32, (count, length), 0) + first
    across = lax.broadcasted_iota(jnp.int32, (count, length), 1)
    picked = jnp.where(down == across, jnp.broadcast_to(row, (count, length)), 0.0)
    return jnp.sum(picked, axis=1, keepdims=True)


def kernel(
    pieces, inner, segments,
    tokens_h, norm_gain_h, final_gain_h, taps_h, rate_h, residue_h,
    embedding, w_in, w_out, fir_state, modal_state, unembed,
    packed_out, fir_new, modal_new,
    product_v, tokens, norm_gain, final_gain, taps, rate, residue,
    emb_v, in_v, out_v, fir_v, modal_v, unembed_v,
    xbuf, fbuf, abuf, arbuf, bbuf, brbuf, zbuf, acc, mixed, squares, state_part, coefs, gated,
    head_acc, scatter, lbuf, ebuf,
    out_state_sem, small_sem, emb_sem, in_sem, out_sem, state_sem, unembed_sem,
    x_send, x_recv, a_send, a_recv, b_send, b_recv, z_send, f_send, f_recv,
    l_send, l_recv, e_send, e_recv,
):
    seg = lax.axis_index("segment")
    me = lax.axis_index("inner")
    last = segments - 1
    chips = inner // 2
    chip = me // 2
    core = me % 2
    steps = tokens.shape[0] - 1
    seqs = tokens.shape[1]
    rows = steps * seqs
    width = emb_v.shape[1]
    sub = width // pieces
    vocab = emb_v.shape[0]
    vocab_local = unembed.shape[1]
    padded = lbuf.shape[2]
    block = seqs // segments
    depth = fir_v.shape[0]
    full = inner * width
    is_short = seg % 2 == 0
    sibling = chip * 2 + (core + 1) % 2

    def member(dx, dc):
        return (chip + dx) % chips * 2 + (core + dc) % 2

    def remote(src, dst, send, recv, where):
        return pltpu.make_async_remote_copy(
            src_ref=src, dst_ref=dst, send_sem=send, recv_sem=recv,
            device_id=where, device_id_type=MESH,
        )

    def arrival(ref, sem):
        pltpu.make_async_copy(ref, ref, sem).wait()

    barrier = pltpu.get_barrier_semaphore()
    for p in range(1, inner):
        pl.semaphore_signal(
            barrier, inc=1, device_id={"inner": member(p // 2, p % 2)}, device_id_type=MESH
        )
    for d in range(1, segments):
        pl.semaphore_signal(
            barrier, inc=1, device_id={"segment": (seg + d) % segments}, device_id_type=MESH
        )

    emb_copy = pltpu.make_async_copy(embedding, emb_v, emb_sem)
    fir_copy = pltpu.make_async_copy(fir_state.at[0], fir_v, state_sem.at[0])
    modal_copy = pltpu.make_async_copy(modal_state.at[0], modal_v, state_sem.at[1])
    unembed_copy = pltpu.make_async_copy(unembed, unembed_v, unembed_sem)
    small = [
        pltpu.make_async_copy(source, target, small_sem.at[index])
        for index, (source, target) in enumerate((
            (tokens_h, tokens), (taps_h, taps), (rate_h, rate), (residue_h, residue),
            (norm_gain_h, norm_gain), (final_gain_h, final_gain),
        ))
    ]

    def in_copy(q, j):
        return pltpu.make_async_copy(
            w_in.at[0, j, pl.ds(pl.multiple_of(q * width, width), width), :],
            in_v.at[q, j],
            in_sem.at[q * 3 + j],
        )

    def out_copy(q, k):
        return pltpu.make_async_copy(
            w_out.at[0, :, pl.ds(pl.multiple_of(q * width + k * sub, sub), sub)],
            out_v.at[q * pieces + k],
            out_sem.at[q * pieces + k],
        )

    small[0].start()

    @pl.when(seg == 0)
    def _():
        emb_copy.start()

    for copy in small[1:]:
        copy.start()

    @pl.when(is_short)
    def _():
        fir_copy.start()

    @pl.when(jnp.logical_not(is_short))
    def _():
        modal_copy.start()

    for t in range(inner):
        for j in range(3):
            in_copy(member(t % chips, t // chips), j).start()

    @pl.loop(0, pieces * inner)
    def _(t):
        out_copy(member(t % chips, (t // chips + 1) % 2), t // inner).start()

    unembed_copy.start()

    @pl.when(is_short)
    def _():
        modal_copy.start()

    @pl.when(jnp.logical_not(is_short))
    def _():
        fir_copy.start()

    fir_whole = pltpu.make_async_copy(fir_v, fir_new, out_state_sem.at[0])
    fir_shift = pltpu.make_async_copy(
        fir_v.at[pl.ds(steps, depth - steps)],
        fir_new.at[pl.ds(0, depth - steps)],
        out_state_sem.at[0],
    )
    fir_latest = pltpu.make_async_copy(
        product_v, fir_new.at[pl.ds(depth - steps, steps)], out_state_sem.at[1]
    )
    modal_done = pltpu.make_async_copy(modal_v, modal_new, out_state_sem.at[2])

    small[0].wait()

    def gather_copy(buf, source, send, recv, k, dx):
        where = sibling if dx == 0 else member(dx, 0)
        return remote(
            source, buf.at[me * pieces + k], send.at[dx * pieces + k],
            recv.at[me * pieces + k], {"inner": where},
        )

    def hand_on(buf, send, recv, k, dx):
        q = member(dx, 0)
        return remote(
            buf.at[q * pieces + k], buf.at[q * pieces + k],
            send.at[(chips + dx) * pieces + k], recv.at[q * pieces + k], {"inner": sibling},
        )

    def x_copy(k, dx):
        return gather_copy(xbuf, xbuf.at[me * pieces + k], x_send, x_recv, k, dx)

    def f_copy(k, dx):
        return gather_copy(fbuf, zbuf.at[k], f_send, f_recv, k, dx)

    def spread(copy_of, k):
        for dx in range(chips - 1, -1, -1):
            copy_of(k, dx).start()

    def pass_on(buf, send, recv):
        for k in range(pieces):
            for dx in range(1, chips):
                q = member(dx, 0)
                arrival(buf.at[q * pieces + k], recv.at[q * pieces + k])
                hand_on(buf, send, recv, k, dx).start()

    @pl.when(seg == 0)
    def _():
        ids = jnp.concatenate(
            [column_of(tokens[pl.ds(t, 1), :].astype(F32), 0, seqs) for t in range(steps)], axis=0
        ).astype(jnp.int32)
        hot = lax.broadcasted_iota(jnp.int32, (rows, vocab), 1) == ids
        hot = hot.astype(F32).astype(BF16)
        emb_copy.wait()
        for k in range(pieces):
            looked_up = jnp.dot(
                hot, emb_v[:, k * sub:(k + 1) * sub], preferred_element_type=F32
            )
            xbuf[me * pieces + k] = looked_up.astype(BF16)

    pl.semaphore_wait(barrier, inner - 1 + segments - 1)

    @pl.when(seg == 0)
    def _():
        for k in range(pieces):
            spread(x_copy, k)

    for copy in small[1:]:
        copy.wait()

    acc[...] = jnp.zeros_like(acc)
    squares[...] = jnp.zeros_like(squares)

    @pl.when(is_short)
    def _():
        fir_copy.wait()
        for t in range(steps):
            coefs[t] = taps[t] if t <= depth else jnp.zeros((1, width), F32)
            for c in range(0, width, 256):
                cols = slice(c, c + 256)
                total = jnp.zeros((seqs, 256), F32)
                for i in range(depth - t):
                    total = total + fir_v[i + t, :, cols] * taps[depth - i, :, cols]
                state_part[t, :, cols] = total

    @pl.when(jnp.logical_not(is_short))
    def _():
        decay = jnp.exp(-rate[0])
        weight = residue[0] * (1.0 - decay)
        for t in range(steps):
            coef = jnp.sum(weight, axis=0, keepdims=True)
            coefs[t] = coef + taps[0] if t == 0 else coef
            weight = weight * decay
        modal_copy.wait()

        @pl.loop(0, seqs)
        def _(b):
            value = modal_v[b]
            for t in range(steps):
                value = value * decay
                state_part[t, pl.ds(b, 1), :] = jnp.sum(value * residue[0], axis=0, keepdims=True)

    def take(values, gain):
        values = values.astype(F32)
        total = squares[...]
        for c in range(0, values.shape[1], 128):
            piece = values[:, c:c + 128]
            total = total + piece * piece
        squares[...] = total
        return (values * gain).astype(BF16)

    def block_of(buf, q):
        return jnp.concatenate([buf[q * pieces + k] for k in range(pieces)], axis=1)

    @pl.when(seg > 0)
    def _():
        for k in range(pieces):
            arrival(xbuf.at[me * pieces + k], x_recv.at[me * pieces + k])
            spread(x_copy, k)

    @pl.loop(0, inner)
    def _(t):
        q = member(t % chips, t // chips)

        @pl.when(t == 1)
        def _():
            pass_on(xbuf, x_send, x_recv)

        @pl.when(t >= chips)
        def _():
            for k in range(pieces):
                arrival(xbuf.at[q * pieces + k], x_recv.at[q * pieces + k])

        offset = pl.multiple_of(q * width, width)
        scaled = take(block_of(xbuf, q), norm_gain[:, pl.ds(offset, width)])
        for j in range(3):
            in_copy(q, j).wait()
            acc[j] += jnp.dot(scaled, in_v[q, j], preferred_element_type=F32)

    scale = lax.rsqrt(jnp.sum(squares[...], axis=1, keepdims=True) / full + EPS)
    for c in range(0, width, sub):
        cols = slice(c, c + sub)
        products = []
        for t in range(steps):
            part = slice(t * seqs, (t + 1) * seqs)
            scale_t = scale[part]
            product = (acc[1, part, cols] * scale_t) * (acc[2, part, cols] * scale_t)
            products.append(product)
            product_v[t, :, cols] = product
            filtered = state_part[t, :, cols]
            for u in range(t + 1):
                filtered = filtered + coefs[t - u, :, cols] * products[u]
            gated[part, cols] = (acc[0, part, cols] * scale_t * filtered).astype(BF16)

    @pl.when(is_short)
    def _():
        fir_shift.start()
        fir_latest.start()

    def a_copy(k):
        return remote(abuf.at[k], arbuf.at[k], a_send.at[k], a_recv.at[k], {"inner": sibling})

    def b_copy(k, dx):
        return remote(
            bbuf.at[dx * pieces + k], brbuf.at[chip * pieces + k], b_send.at[dx * pieces + k],
            b_recv.at[chip * pieces + k], {"inner": member(dx, 0)},
        )

    def z_copy(k):
        return remote(
            zbuf.at[k], xbuf.at[me * pieces + k], z_send.at[k],
            x_recv.at[me * pieces + k], {"segment": (seg + 1) % segments},
        )

    def mix(q, k):
        out_copy(q, k).wait()
        return jnp.dot(gated[...], out_v[q * pieces + k], preferred_element_type=F32)

    @pl.loop(0, pieces)
    def _(k):
        for x in range(chips):
            abuf[k, x] = mix(x * 2 + (core + 1) % 2, k).astype(BF16)
        a_copy(k).start()

    @pl.loop(0, pieces)
    def _(k):
        for dx in range(1, chips):
            mixed[k, dx] = mix(member(dx, 0), k)

    @pl.loop(0, pieces)
    def _(k):
        arrival(arbuf.at[k], a_recv.at[k])
        for dx in range(chips - 1, 0, -1):
            total = mixed[k, dx] + arbuf[k, (chip + dx) % chips].astype(F32)
            bbuf[dx * pieces + k] = total.astype(BF16)
            b_copy(k, dx).start()

    @pl.loop(0, pieces)
    def _(k):
        total = mix(me, k) + arbuf[k, chip].astype(F32)
        mixed[k, 0] = total + xbuf[me * pieces + k].astype(F32)

    @pl.loop(0, pieces)
    def _(k):
        total = mixed[k, 0]
        for dx in range(1, chips):
            source = (chip + dx) % chips * pieces + k
            arrival(brbuf.at[source], b_recv.at[source])
            total = total + brbuf[source].astype(F32)
        zbuf[k] = total.astype(BF16)

        @pl.when(seg < last)
        def _():
            z_copy(k).start()

        @pl.when(seg == last)
        def _():
            spread(f_copy, k)

    @pl.when(is_short)
    def _():
        modal_copy.wait()

    @pl.when(jnp.logical_not(is_short))
    def _():
        fir_copy.wait()
        fir_whole.start()
        decay = jnp.exp(-rate[0])

        @pl.loop(0, seqs)
        def _(b):
            value = modal_v[b]
            for t in range(steps):
                value = decay * value + (1.0 - decay) * product_v[t, pl.ds(b, 1), :]
            modal_v[b] = value

    modal_done.start()

    unembed_copy.wait()

    def l_copy(s):
        return remote(scatter.at[s], lbuf, l_send.at[s], l_recv, {"segment": s})

    @pl.when(seg == last)
    def _():
        squares[...] = jnp.zeros_like(squares)
        head_acc[...] = jnp.zeros_like(head_acc)

        def head(values, q):
            offset = pl.multiple_of(q * width, width)
            scaled = take(values, final_gain[:, pl.ds(offset, width)])
            head_acc[:, :vocab_local] += jnp.dot(
                scaled, unembed_v[pl.ds(offset, width), :], preferred_element_type=F32
            )

        head(jnp.concatenate([zbuf[k] for k in range(pieces)], axis=1), me)
        pass_on(fbuf, f_send, f_recv)

        @pl.loop(1, inner)
        def _(t):
            q = member(t % chips, t // chips)

            @pl.when(t >= chips)
            def _():
                for k in range(pieces):
                    arrival(fbuf.at[q * pieces + k], f_recv.at[q * pieces + k])

            head(block_of(fbuf, q), q)

        final_scale = lax.rsqrt(jnp.sum(squares[...], axis=1, keepdims=True) / full + EPS)
        logits = head_acc[...] * final_scale
        for s in range(segments):
            for t in range(steps):
                start = t * seqs + s * block
                if s < last:
                    scatter[s, t] = logits[start:start + block]
                else:
                    lbuf[t] = logits[start:start + block]
            if s < last:
                l_copy(s).start()

    @pl.when(seg < last)
    def _():
        arrival(lbuf, l_recv)

    def e_copy(p):
        return remote(
            ebuf.at[me], ebuf.at[me], e_send.at[p], e_recv.at[me],
            {"inner": member(p // 2, p % 2)},
        )

    columns = lax.broadcasted_iota(jnp.int32, (block, vocab_local), 1) + me * vocab_local
    lanes = lax.broadcasted_iota(jnp.int32, (block, 128), 1)
    for t in range(steps):
        logits_t = lbuf[t, :, :vocab_local]
        packed_out[t, :, :vocab_local] = logits_t
        target = column_of(tokens[pl.ds(t + 1, 1), :].astype(F32), seg * block, block)
        hit = columns == target.astype(jnp.int32)
        exp_sum = jnp.sum(jnp.exp(logits_t), axis=1, keepdims=True)
        target_part = jnp.sum(jnp.where(hit, logits_t, 0.0), axis=1, keepdims=True)
        ebuf[me, t] = jnp.where(lanes == 0, exp_sum, target_part)
    for p in range(inner - 1, 0, -1):
        e_copy(p).start()
    sums = ebuf[me]
    for p in range(1, inner):
        q = member(p // 2, p % 2)
        arrival(ebuf.at[q], e_recv.at[q])
        sums = sums + ebuf[q]
    for t in range(steps):
        logprob = sums[t, :, 1:2] - jnp.log(sums[t, :, 0:1])
        packed_out[t, :, padded:] = jnp.broadcast_to(logprob, (block, 128))

    @pl.when(is_short)
    def _():
        fir_shift.wait()
        fir_latest.wait()

    @pl.when(jnp.logical_not(is_short))
    def _():
        fir_whole.wait()

    modal_done.wait()

    @pl.loop(0, pieces)
    def _(k):
        a_copy(k).wait_send()
        for dx in range(chips):
            x_copy(k, dx).wait_send()
            if dx > 0:
                hand_on(xbuf, x_send, x_recv, k, dx).wait_send()
                b_copy(k, dx).wait_send()

        @pl.when(seg < last)
        def _():
            z_copy(k).wait_send()

        @pl.when(seg == last)
        def _():
            for dx in range(chips):
                f_copy(k, dx).wait_send()
                if dx > 0:
                    hand_on(fbuf, f_send, f_recv, k, dx).wait_send()

    @pl.when(seg == last)
    def _():
        for s in range(segments - 1):
            l_copy(s).wait_send()

    for p in range(1, inner):
        e_copy(p).wait_send()


def hand_out(
    vocab_local, padded, packed, fir_new, modal_new, logits, logprob, fir, modal,
    fir_v, modal_v, in_sems, out_sems,
):
    parts = [(fir_new, fir_v, fir, i) for i in range(fir_v.shape[0])]
    share = modal_v.shape[0] // 4
    parts += [(modal_new, modal_v, modal, pl.ds(i * share, share)) for i in range(4)]
    arriving = [
        pltpu.make_async_copy(source.at[where], held.at[where], in_sems.at[i])
        for i, (source, held, _, where) in enumerate(parts)
    ]
    leaving = [
        pltpu.make_async_copy(held.at[where], target.at[0, where], out_sems.at[i])
        for i, (_, held, target, where) in enumerate(parts)
    ]
    for copy in arriving:
        copy.start()
    steps, block = logprob.shape
    down = lax.broadcasted_iota(jnp.int32, (block, block), 0)
    across = lax.broadcasted_iota(jnp.int32, (block, block), 1)
    for t in range(steps):
        logits[t] = packed[t, :, :vocab_local]
        spread_out = packed[t, :, padded:padded + block]
        logprob[t:t + 1, :] = jnp.sum(
            jnp.where(down == across, spread_out, 0.0), axis=0, keepdims=True
        )
    for before, after in zip(arriving, leaving):
        before.wait()
        after.start()
    for copy in leaving:
        copy.wait()


def per_device(
    inner, segments, tokens, embedding, in_proj, out_proj, norm_gain, fir_taps, modal_rate,
    modal_residue, fir_state, modal_state, final_gain, unembed,
):
    steps = tokens.shape[0] - 1
    seqs = tokens.shape[1]
    rows = steps * seqs
    vocab, width = embedding.shape
    pieces = max(1, width // 256)
    sub = width // pieces
    chips = inner // 2
    full = inner * width
    vocab_local = unembed.shape[1]
    padded = max(128, vocab_local)
    block = seqs // segments
    whole = pl.BlockSpec(memory_space=pltpu.VMEM)
    in_hbm = pl.BlockSpec(memory_space=pltpu.HBM)
    dma = pltpu.SemaphoreType.DMA
    fir_by_tap = jnp.transpose(fir_state, (0, 2, 1, 3))
    operands = (
        tokens, norm_gain, final_gain[None], jnp.transpose(fir_taps, (1, 0, 2)), modal_rate,
        modal_residue, embedding, in_proj, out_proj, fir_by_tap, modal_state, unembed,
    )
    packed, fir_new, modal_new = pl.pallas_call(
        functools.partial(kernel, pieces, inner, segments),
        out_shape=(
            jax.ShapeDtypeStruct((steps, block, padded + 128), F32),
            jax.ShapeDtypeStruct(fir_by_tap.shape[1:], F32),
            jax.ShapeDtypeStruct(modal_state.shape[1:], F32),
        ),
        in_specs=[in_hbm] * len(operands),
        out_specs=(whole, in_hbm, in_hbm),
        scratch_shapes=[
            pltpu.VMEM((steps, seqs, width), F32),
            *[pltpu.VMEM(o.shape, o.dtype) for o in operands[:6]],
            pltpu.VMEM((vocab, width), BF16),
            pltpu.VMEM((inner, 3, width, width), BF16),
            pltpu.VMEM((inner * pieces, width, sub), BF16),
            pltpu.VMEM(fir_by_tap.shape[1:], F32),
            pltpu.VMEM(modal_state.shape[1:], F32),
            pltpu.VMEM((full, vocab_local), BF16),
            pltpu.VMEM((inner * pieces, rows, sub), BF16),
            pltpu.VMEM((inner * pieces, rows, sub), BF16),
            pltpu.VMEM((pieces, chips, rows, sub), BF16),
            pltpu.VMEM((pieces, chips, rows, sub), BF16),
            pltpu.VMEM((chips * pieces, rows, sub), BF16),
            pltpu.VMEM((chips * pieces, rows, sub), BF16),
            pltpu.VMEM((pieces, rows, sub), BF16),
            pltpu.VMEM((3, rows, width), F32),
            pltpu.VMEM((pieces, chips, rows, sub), F32),
            pltpu.VMEM((rows, 128), F32),
            pltpu.VMEM((steps, seqs, width), F32),
            pltpu.VMEM((steps, 1, width), F32),
            pltpu.VMEM((rows, width), BF16),
            pltpu.VMEM((rows, padded), F32),
            pltpu.VMEM((segments, steps, block, padded), F32),
            pltpu.VMEM((steps, block, padded), F32),
            pltpu.VMEM((inner, steps, block, 128), F32),
            dma((3,)),
            dma((6,)),
            dma,
            dma((inner * 3,)),
            dma((inner * pieces,)),
            dma((2,)),
            dma,
            dma((inner * pieces,)),
            dma((inner * pieces,)),
            dma((pieces,)),
            dma((pieces,)),
            dma((chips * pieces,)),
            dma((chips * pieces,)),
            dma((pieces,)),
            dma((inner * pieces,)),
            dma((inner * pieces,)),
            dma((segments,)),
            dma,
            dma((inner,)),
            dma((inner,)),
        ],
        compiler_params=pltpu.CompilerParams(
            collective_id=0, has_side_effects=True, vmem_limit_bytes=60 * 1024 * 1024
        ),
    )(*operands)
    logits, logprob, fir_out, modal_out = pl.pallas_call(
        functools.partial(hand_out, vocab_local, padded),
        out_shape=(
            jax.ShapeDtypeStruct((steps, block, vocab_local), F32),
            jax.ShapeDtypeStruct((steps, block), F32),
            jax.ShapeDtypeStruct(fir_by_tap.shape, F32),
            jax.ShapeDtypeStruct(modal_state.shape, F32),
        ),
        in_specs=[whole, in_hbm, in_hbm],
        out_specs=(whole, whole, in_hbm, in_hbm),
        scratch_shapes=[
            pltpu.VMEM(fir_new.shape, F32),
            pltpu.VMEM(modal_new.shape, F32),
            dma((fir_new.shape[0] + 4,)),
            dma((fir_new.shape[0] + 4,)),
        ],
        compiler_params=pltpu.CompilerParams(vmem_limit_bytes=60 * 1024 * 1024),
    )(packed, fir_new, modal_new)
    return (logits, logprob, jnp.transpose(fir_out, (0, 2, 1, 3)), modal_out)


def solution(mesh):
    inner = mesh.shape["inner"]
    segments = mesh.shape["segment"]
    return jax.shard_map(
        functools.partial(per_device, inner, segments),
        mesh=mesh,
        in_specs=(
            P(None, "groups"),
            P(None, "inner"),
            P("segment", None, None, "inner"),
            P("segment", "inner", None),
            P("segment", None),
            P("segment", None, "inner"),
            P("segment", None, "inner"),
            P("segment", None, "inner"),
            P("segment", "groups", None, "inner"),
            P("segment", "groups", None, "inner"),
            P(),
            P(None, "inner"),
        ),
        out_specs=(
            P(None, ("groups", "segment"), "inner"),
            P(None, ("groups", "segment")),
            P("segment", "groups", None, "inner"),
            P("segment", "groups", None, "inner"),
        ),
        check_vma=False,
    )
```

```python
import functools

import jax
import jax.numpy as jnp
from jax import lax
from jax.experimental import pallas as pl
from jax.experimental.pallas import tpu as pltpu
from jax.sharding import PartitionSpec as P

EPS = 1e-05
MESH = pl.DeviceIdType.MESH
F32 = jnp.float32
BF16 = jnp.bfloat16


def column_of(row, first, count):
    length = row.shape[1]
    down = lax.broadcasted_iota(jnp.int32, (count, length), 0) + first
    across = lax.broadcasted_iota(jnp.int32, (count, length), 1)
    picked = jnp.where(down == across, jnp.broadcast_to(row, (count, length)), 0.0)
    return jnp.sum(picked, axis=1, keepdims=True)


def kernel(
    pieces, inner, segments,
    tokens_h, norm_gain_h, final_gain_h, taps_h, rate_h, residue_h,
    embedding, w_in, w_out, fir_state, modal_state, unembed,
    packed_out, fir_new, modal_new,
    product_v, tokens, norm_gain, final_gain, taps, rate, residue,
    emb_v, in_v, out_v, fir_v, modal_v, unembed_v,
    xbuf, fbuf, abuf, arbuf, bbuf, brbuf, zbuf, acc, mixed, squares, state_part, coefs, gated,
    head_acc, scatter, lbuf, ebuf,
    out_state_sem, small_sem, emb_sem, in_sem, out_sem, state_sem, unembed_sem,
    x_send, x_recv, a_send, a_recv, b_send, b_recv, z_send, f_send, f_recv,
    l_send, l_recv, e_send, e_recv,
):
    seg = lax.axis_index("segment")
    me = lax.axis_index("inner")
    last = segments - 1
    chips = inner // 2
    chip = me // 2
    core = me % 2
    steps = tokens.shape[0] - 1
    seqs = tokens.shape[1]
    rows = steps * seqs
    width = emb_v.shape[1]
    sub = width // pieces
    vocab = emb_v.shape[0]
    vocab_local = unembed.shape[1]
    padded = lbuf.shape[2]
    block = seqs // segments
    depth = fir_v.shape[0]
    full = inner * width
    is_short = seg % 2 == 0
    sibling = chip * 2 + (core + 1) % 2

    def member(dx, dc):
        return (chip + dx) % chips * 2 + (core + dc) % 2

    def remote(src, dst, send, recv, where):
        return pltpu.make_async_remote_copy(
            src_ref=src, dst_ref=dst, send_sem=send, recv_sem=recv,
            device_id=where, device_id_type=MESH,
        )

    def arrival(ref, sem):
        pltpu.make_async_copy(ref, ref, sem).wait()

    barrier = pltpu.get_barrier_semaphore()
    for p in range(1, inner):
        pl.semaphore_signal(
            barrier, inc=1, device_id={"inner": member(p // 2, p % 2)}, device_id_type=MESH
        )
    for d in range(1, segments):
        pl.semaphore_signal(
            barrier, inc=1, device_id={"segment": (seg + d) % segments}, device_id_type=MESH
        )

    emb_copy = pltpu.make_async_copy(embedding, emb_v, emb_sem)
    fir_copy = pltpu.make_async_copy(fir_state.at[0], fir_v, state_sem.at[0])
    modal_copy = pltpu.make_async_copy(modal_state.at[0], modal_v, state_sem.at[1])
    unembed_copy = pltpu.make_async_copy(unembed, unembed_v, unembed_sem)
    small = [
        pltpu.make_async_copy(source, target, small_sem.at[index])
        for index, (source, target) in enumerate((
            (tokens_h, tokens), (taps_h, taps), (rate_h, rate), (residue_h, residue),
            (norm_gain_h, norm_gain), (final_gain_h, final_gain),
        ))
    ]

    def in_copy(q, j):
        return pltpu.make_async_copy(
            w_in.at[0, j, pl.ds(pl.multiple_of(q * width, width), width), :],
            in_v.at[q, j],
            in_sem.at[q * 3 + j],
        )

    def out_copy(q, k):
        return pltpu.make_async_copy(
            w_out.at[0, :, pl.ds(pl.multiple_of(q * width + k * sub, sub), sub)],
            out_v.at[q * pieces + k],
            out_sem.at[q * pieces + k],
        )

    small[0].start()

    @pl.when(seg == 0)
    def _():
        emb_copy.start()

    for copy in small[1:]:
        copy.start()

    @pl.when(is_short)
    def _():
        fir_copy.start()

    @pl.when(jnp.logical_not(is_short))
    def _():
        modal_copy.start()

    for t in range(inner):
        for j in range(3):
            in_copy(member(t % chips, t // chips), j).start()

    @pl.loop(0, pieces * inner)
    def _(t):
        out_copy(member(t % chips, (t // chips + 1) % 2), t // inner).start()

    unembed_copy.start()

    @pl.when(is_short)
    def _():
        modal_copy.start()

    @pl.when(jnp.logical_not(is_short))
    def _():
        fir_copy.start()

    fir_whole = pltpu.make_async_copy(fir_v, fir_new, out_state_sem.at[0])
    fir_shift = pltpu.make_async_copy(
        fir_v.at[pl.ds(steps, depth - steps)],
        fir_new.at[pl.ds(0, depth - steps)],
        out_state_sem.at[0],
    )
    fir_latest = pltpu.make_async_copy(
        product_v, fir_new.at[pl.ds(depth - steps, steps)], out_state_sem.at[1]
    )
    modal_done = pltpu.make_async_copy(modal_v, modal_new, out_state_sem.at[2])

    small[0].wait()

    def gather_copy(buf, source, send, recv, k, dx):
        where = sibling if dx == 0 else member(dx, 0)
        return remote(
            source, buf.at[me * pieces + k], send.at[dx * pieces + k],
            recv.at[me * pieces + k], {"inner": where},
        )

    def hand_on(buf, send, recv, k, dx):
        q = member(dx, 0)
        return remote(
            buf.at[q * pieces + k], buf.at[q * pieces + k],
            send.at[(chips + dx) * pieces + k], recv.at[q * pieces + k], {"inner": sibling},
        )

    def x_copy(k, dx):
        return gather_copy(xbuf, xbuf.at[me * pieces + k], x_send, x_recv, k, dx)

    def f_copy(k, dx):
        return gather_copy(fbuf, zbuf.at[k], f_send, f_recv, k, dx)

    def spread(copy_of, k):
        for dx in range(chips - 1, -1, -1):
            copy_of(k, dx).start()

    def pass_on(buf, send, recv):
        for k in range(pieces):
            for dx in range(1, chips):
                q = member(dx, 0)
                arrival(buf.at[q * pieces + k], recv.at[q * pieces + k])
                hand_on(buf, send, recv, k, dx).start()

    @pl.when(seg == 0)
    def _():
        ids = jnp.concatenate(
            [column_of(tokens[pl.ds(t, 1), :].astype(F32), 0, seqs) for t in range(steps)], axis=0
        ).astype(jnp.int32)
        hot = lax.broadcasted_iota(jnp.int32, (rows, vocab), 1) == ids
        hot = hot.astype(F32).astype(BF16)
        emb_copy.wait()
        for k in range(pieces):
            looked_up = jnp.dot(
                hot, emb_v[:, k * sub:(k + 1) * sub], preferred_element_type=F32
            )
            xbuf[me * pieces + k] = looked_up.astype(BF16)

    pl.semaphore_wait(barrier, inner - 1 + segments - 1)

    @pl.when(seg == 0)
    def _():
        for k in range(pieces):
            spread(x_copy, k)

    for copy in small[1:]:
        copy.wait()

    acc[...] = jnp.zeros_like(acc)
    squares[...] = jnp.zeros_like(squares)

    @pl.when(is_short)
    def _():
        fir_copy.wait()
        for t in range(steps):
            coefs[t] = taps[t] if t <= depth else jnp.zeros((1, width), F32)
            for c in range(0, width, 256):
                cols = slice(c, c + 256)
                total = jnp.zeros((seqs, 256), F32)
                for i in range(depth - t):
                    total = total + fir_v[i + t, :, cols] * taps[depth - i, :, cols]
                state_part[t, :, cols] = total

    @pl.when(jnp.logical_not(is_short))
    def _():
        decay = jnp.exp(-rate[0])
        weight = residue[0] * (1.0 - decay)
        for t in range(steps):
            coef = jnp.sum(weight, axis=0, keepdims=True)
            coefs[t] = coef + taps[0] if t == 0 else coef
            weight = weight * decay
        modal_copy.wait()

        @pl.loop(0, seqs)
        def _(b):
            value = modal_v[b]
            for t in range(steps):
                value = value * decay
                state_part[t, pl.ds(b, 1), :] = jnp.sum(value * residue[0], axis=0, keepdims=True)

    def take(values, gain):
        values = values.astype(F32)
        total = squares[...]
        for c in range(0, values.shape[1], 128):
            piece = values[:, c:c + 128]
            total = total + piece * piece
        squares[...] = total
        return (values * gain).astype(BF16)

    def block_of(buf, q):
        return jnp.concatenate([buf[q * pieces + k] for k in range(pieces)], axis=1)

    @pl.when(seg > 0)
    def _():
        for k in range(pieces):
            arrival(xbuf.at[me * pieces + k], x_recv.at[me * pieces + k])
            spread(x_copy, k)

    @pl.loop(0, inner)
    def _(t):
        q = member(t % chips, t // chips)

        @pl.when(t == 1)
        def _():
            pass_on(xbuf, x_send, x_recv)

        @pl.when(t >= chips)
        def _():
            for k in range(pieces):
                arrival(xbuf.at[q * pieces + k], x_recv.at[q * pieces + k])

        offset = pl.multiple_of(q * width, width)
        scaled = take(block_of(xbuf, q), norm_gain[:, pl.ds(offset, width)])
        for j in range(3):
            in_copy(q, j).wait()
            acc[j] += jnp.dot(scaled, in_v[q, j], preferred_element_type=F32)

    scale = lax.rsqrt(jnp.sum(squares[...], axis=1, keepdims=True) / full + EPS)
    for c in range(0, width, sub):
        cols = slice(c, c + sub)
        products = []
        for t in range(steps):
            part = slice(t * seqs, (t + 1) * seqs)
            scale_t = scale[part]
            product = (acc[1, part, cols] * scale_t) * (acc[2, part, cols] * scale_t)
            products.append(product)
            product_v[t, :, cols] = product
            filtered = state_part[t, :, cols]
            for u in range(t + 1):
                filtered = filtered + coefs[t - u, :, cols] * products[u]
            gated[part, cols] = (acc[0, part, cols] * scale_t * filtered).astype(BF16)

    @pl.when(is_short)
    def _():
        fir_shift.start()
        fir_latest.start()

    def a_copy(k):
        return remote(abuf.at[k], arbuf.at[k], a_send.at[k], a_recv.at[k], {"inner": sibling})

    def b_copy(k, dx):
        return remote(
            bbuf.at[dx * pieces + k], brbuf.at[chip * pieces + k], b_send.at[dx * pieces + k],
            b_recv.at[chip * pieces + k], {"inner": member(dx, 0)},
        )

    def z_copy(k):
        return remote(
            zbuf.at[k], xbuf.at[me * pieces + k], z_send.at[k],
            x_recv.at[me * pieces + k], {"segment": (seg + 1) % segments},
        )

    def mix(q, k):
        out_copy(q, k).wait()
        return jnp.dot(gated[...], out_v[q * pieces + k], preferred_element_type=F32)

    @pl.loop(0, pieces)
    def _(k):
        @pl.loop(0, chips)
        def _(x):
            abuf[k, x] = mix(x * 2 + (core + 1) % 2, k).astype(BF16)

        a_copy(k).start()

    @pl.loop(0, pieces)
    def _(k):
        for dx in range(chips - 1, -1, -1):
            mixed[dx] = mix(member(dx, 0), k)
        arrival(arbuf.at[k], a_recv.at[k])
        for dx in range(chips - 1, 0, -1):
            total = mixed[dx] + arbuf[k, (chip + dx) % chips].astype(F32)
            bbuf[dx * pieces + k] = total.astype(BF16)
            b_copy(k, dx).start()
        total = mixed[0] + arbuf[k, chip].astype(F32)
        acc[0, :, pl.ds(pl.multiple_of(k * sub, sub), sub)] = (
            total + xbuf[me * pieces + k].astype(F32)
        )

    @pl.loop(0, pieces)
    def _(k):
        total = acc[0, :, pl.ds(pl.multiple_of(k * sub, sub), sub)]
        for dx in range(1, chips):
            source = (chip + dx) % chips * pieces + k
            arrival(brbuf.at[source], b_recv.at[source])
            total = total + brbuf[source].astype(F32)
        zbuf[k] = total.astype(BF16)

        @pl.when(seg < last)
        def _():
            z_copy(k).start()

        @pl.when(seg == last)
        def _():
            spread(f_copy, k)

    def finish_states():
        @pl.when(is_short)
        def _():
            modal_copy.wait()

        @pl.when(jnp.logical_not(is_short))
        def _():
            fir_copy.wait()
            fir_whole.start()
            decay = jnp.exp(-rate[0])

            @pl.loop(0, seqs)
            def _(b):
                value = modal_v[b]
                for t in range(steps):
                    value = decay * value + (1.0 - decay) * product_v[t, pl.ds(b, 1), :]
                modal_v[b] = value

        modal_done.start()

    unembed_copy.wait()

    def l_copy(s):
        return remote(scatter.at[s], lbuf, l_send.at[s], l_recv, {"segment": s})

    @pl.when(seg == last)
    def _():
        squares[...] = jnp.zeros_like(squares)
        head_acc[...] = jnp.zeros_like(head_acc)

        def head(values, q):
            offset = pl.multiple_of(q * width, width)
            scaled = take(values, final_gain[:, pl.ds(offset, width)])
            head_acc[:, :vocab_local] += jnp.dot(
                scaled, unembed_v[pl.ds(offset, width), :], preferred_element_type=F32
            )

        head(jnp.concatenate([zbuf[k] for k in range(pieces)], axis=1), me)
        pass_on(fbuf, f_send, f_recv)

        @pl.loop(1, inner)
        def _(t):
            q = member(t % chips, t // chips)

            @pl.when(t >= chips)
            def _():
                for k in range(pieces):
                    arrival(fbuf.at[q * pieces + k], f_recv.at[q * pieces + k])

            head(block_of(fbuf, q), q)

        final_scale = lax.rsqrt(jnp.sum(squares[...], axis=1, keepdims=True) / full + EPS)
        logits = head_acc[...] * final_scale
        for s in range(segments):
            for t in range(steps):
                start = t * seqs + s * block
                if s < last:
                    scatter[s, t] = logits[start:start + block]
                else:
                    lbuf[t] = logits[start:start + block]
            if s < last:
                l_copy(s).start()

    @pl.when(seg < last)
    def _():
        finish_states()
        arrival(lbuf, l_recv)

    def e_copy(p):
        return remote(
            ebuf.at[me], ebuf.at[me], e_send.at[p], e_recv.at[me],
            {"inner": member(p // 2, p % 2)},
        )

    columns = lax.broadcasted_iota(jnp.int32, (block, vocab_local), 1) + me * vocab_local
    lanes = lax.broadcasted_iota(jnp.int32, (block, 128), 1)
    for t in range(steps):
        logits_t = lbuf[t, :, :vocab_local]
        packed_out[t, :, :vocab_local] = logits_t
        target = column_of(tokens[pl.ds(t + 1, 1), :].astype(F32), seg * block, block)
        hit = columns == target.astype(jnp.int32)
        exp_sum = jnp.sum(jnp.exp(logits_t), axis=1, keepdims=True)
        target_part = jnp.sum(jnp.where(hit, logits_t, 0.0), axis=1, keepdims=True)
        ebuf[me, t] = jnp.where(lanes == 0, exp_sum, target_part)
    for p in range(inner - 1, 0, -1):
        e_copy(p).start()

    @pl.when(seg == last)
    def _():
        finish_states()

    sums = ebuf[me]
    for p in range(1, inner):
        q = member(p // 2, p % 2)
        arrival(ebuf.at[q], e_recv.at[q])
        sums = sums + ebuf[q]
    for t in range(steps):
        logprob = sums[t, :, 1:2] - jnp.log(sums[t, :, 0:1])
        packed_out[t, :, padded:] = jnp.broadcast_to(logprob, (block, 128))

    @pl.when(is_short)
    def _():
        fir_shift.wait()
        fir_latest.wait()

    @pl.when(jnp.logical_not(is_short))
    def _():
        fir_whole.wait()

    modal_done.wait()

    @pl.loop(0, pieces)
    def _(k):
        a_copy(k).wait_send()
        for dx in range(chips):
            x_copy(k, dx).wait_send()
            if dx > 0:
                hand_on(xbuf, x_send, x_recv, k, dx).wait_send()
                b_copy(k, dx).wait_send()

        @pl.when(seg < last)
        def _():
            z_copy(k).wait_send()

        @pl.when(seg == last)
        def _():
            for dx in range(chips):
                f_copy(k, dx).wait_send()
                if dx > 0:
                    hand_on(fbuf, f_send, f_recv, k, dx).wait_send()

    @pl.when(seg == last)
    def _():
        for s in range(segments - 1):
            l_copy(s).wait_send()

    for p in range(1, inner):
        e_copy(p).wait_send()


def hand_out(
    vocab_local, padded, packed, fir_new, modal_new, logits, logprob, fir, modal,
    packed_v, logits_v, logprob_v, fir_v, modal_v, in_sems, out_sems,
):
    half = fir_v.shape[0] // 2
    share = modal_v.shape[0] // 2
    parts = [(fir_new, fir_v, fir, pl.ds(i * half, half)) for i in range(2)]
    parts += [(modal_new, modal_v, modal, pl.ds(i * share, share)) for i in range(2)]
    packed_copy = pltpu.make_async_copy(packed, packed_v, in_sems.at[4])
    logits_copy = pltpu.make_async_copy(logits_v, logits, out_sems.at[4])
    logprob_copy = pltpu.make_async_copy(logprob_v, logprob, out_sems.at[5])
    arriving = [
        pltpu.make_async_copy(source.at[where], held.at[where], in_sems.at[i])
        for i, (source, held, _, where) in enumerate(parts)
    ]
    leaving = [
        pltpu.make_async_copy(held.at[where], target.at[0, where], out_sems.at[i])
        for i, (_, held, target, where) in enumerate(parts)
    ]
    packed_copy.start()
    for copy in arriving:
        copy.start()
    packed_copy.wait()
    steps, block = logprob.shape
    down = lax.broadcasted_iota(jnp.int32, (block, block), 0)
    across = lax.broadcasted_iota(jnp.int32, (block, block), 1)
    for t in range(steps):
        logits_v[t] = packed_v[t, :, :vocab_local]
        spread_out = packed_v[t, :, padded:padded + block]
        logprob_v[t:t + 1, :] = jnp.sum(
            jnp.where(down == across, spread_out, 0.0), axis=0, keepdims=True
        )
    logits_copy.start()
    logprob_copy.start()
    for before, after in zip(arriving, leaving):
        before.wait()
        after.start()
    for copy in leaving:
        copy.wait()
    logits_copy.wait()
    logprob_copy.wait()


def per_device(
    inner, segments, tokens, embedding, in_proj, out_proj, norm_gain, fir_taps, modal_rate,
    modal_residue, fir_state, modal_state, final_gain, unembed,
):
    steps = tokens.shape[0] - 1
    seqs = tokens.shape[1]
    rows = steps * seqs
    vocab, width = embedding.shape
    pieces = max(1, width // 256)
    sub = width // pieces
    chips = inner // 2
    full = inner * width
    vocab_local = unembed.shape[1]
    padded = max(128, vocab_local)
    block = seqs // segments
    whole = pl.BlockSpec(memory_space=pltpu.VMEM)
    in_hbm = pl.BlockSpec(memory_space=pltpu.HBM)
    dma = pltpu.SemaphoreType.DMA
    fir_by_tap = jnp.transpose(fir_state, (0, 2, 1, 3))
    operands = (
        tokens, norm_gain, final_gain[None], jnp.transpose(fir_taps, (1, 0, 2)), modal_rate,
        modal_residue, embedding, in_proj, out_proj, fir_by_tap, modal_state, unembed,
    )
    packed, fir_new, modal_new = pl.pallas_call(
        functools.partial(kernel, pieces, inner, segments),
        out_shape=(
            jax.ShapeDtypeStruct((steps, block, padded + 128), F32),
            jax.ShapeDtypeStruct(fir_by_tap.shape[1:], F32),
            jax.ShapeDtypeStruct(modal_state.shape[1:], F32),
        ),
        in_specs=[in_hbm] * len(operands),
        out_specs=(whole, in_hbm, in_hbm),
        scratch_shapes=[
            pltpu.VMEM((steps, seqs, width), F32),
            *[pltpu.VMEM(o.shape, o.dtype) for o in operands[:6]],
            pltpu.VMEM((vocab, width), BF16),
            pltpu.VMEM((inner, 3, width, width), BF16),
            pltpu.VMEM((inner * pieces, width, sub), BF16),
            pltpu.VMEM(fir_by_tap.shape[1:], F32),
            pltpu.VMEM(modal_state.shape[1:], F32),
            pltpu.VMEM((full, vocab_local), BF16),
            pltpu.VMEM((inner * pieces, rows, sub), BF16),
            pltpu.VMEM((inner * pieces, rows, sub), BF16),
            pltpu.VMEM((pieces, chips, rows, sub), BF16),
            pltpu.VMEM((pieces, chips, rows, sub), BF16),
            pltpu.VMEM((chips * pieces, rows, sub), BF16),
            pltpu.VMEM((chips * pieces, rows, sub), BF16),
            pltpu.VMEM((pieces, rows, sub), BF16),
            pltpu.VMEM((3, rows, width), F32),
            pltpu.VMEM((chips, rows, sub), F32),
            pltpu.VMEM((rows, 128), F32),
            pltpu.VMEM((steps, seqs, width), F32),
            pltpu.VMEM((steps, 1, width), F32),
            pltpu.VMEM((rows, width), BF16),
            pltpu.VMEM((rows, padded), F32),
            pltpu.VMEM((segments, steps, block, padded), F32),
            pltpu.VMEM((steps, block, padded), F32),
            pltpu.VMEM((inner, steps, block, 128), F32),
            dma((3,)),
            dma((6,)),
            dma,
            dma((inner * 3,)),
            dma((inner * pieces,)),
            dma((2,)),
            dma,
            dma((inner * pieces,)),
            dma((inner * pieces,)),
            dma((pieces,)),
            dma((pieces,)),
            dma((chips * pieces,)),
            dma((chips * pieces,)),
            dma((pieces,)),
            dma((inner * pieces,)),
            dma((inner * pieces,)),
            dma((segments,)),
            dma,
            dma((inner,)),
            dma((inner,)),
        ],
        compiler_params=pltpu.CompilerParams(
            collective_id=0, has_side_effects=True, vmem_limit_bytes=60 * 1024 * 1024
        ),
    )(*operands)
    logits, logprob, fir_out, modal_out = pl.pallas_call(
        functools.partial(hand_out, vocab_local, padded),
        out_shape=(
            jax.ShapeDtypeStruct((steps, block, vocab_local), F32),
            jax.ShapeDtypeStruct((steps, block), F32),
            jax.ShapeDtypeStruct(fir_by_tap.shape, F32),
            jax.ShapeDtypeStruct(modal_state.shape, F32),
        ),
        in_specs=[in_hbm] * 3,
        out_specs=(in_hbm,) * 4,
        scratch_shapes=[
            pltpu.VMEM(packed.shape, F32),
            pltpu.VMEM((steps, block, vocab_local), F32),
            pltpu.VMEM((steps, block), F32),
            pltpu.VMEM(fir_new.shape, F32),
            pltpu.VMEM(modal_new.shape, F32),
            dma((5,)),
            dma((6,)),
        ],
        compiler_params=pltpu.CompilerParams(vmem_limit_bytes=60 * 1024 * 1024),
    )(packed, fir_new, modal_new)
    return (logits, logprob, jnp.transpose(fir_out, (0, 2, 1, 3)), modal_out)


def solution(mesh):
    inner = mesh.shape["inner"]
    segments = mesh.shape["segment"]
    return jax.shard_map(
        functools.partial(per_device, inner, segments),
        mesh=mesh,
        in_specs=(
            P(None, "groups"),
            P(None, "inner"),
            P("segment", None, None, "inner"),
            P("segment", "inner", None),
            P("segment", None),
            P("segment", None, "inner"),
            P("segment", None, "inner"),
            P("segment", None, "inner"),
            P("segment", "groups", None, "inner"),
            P("segment", "groups", None, "inner"),
            P(),
            P(None, "inner"),
        ),
        out_specs=(
            P(None, ("groups", "segment"), "inner"),
            P(None, ("groups", "segment")),
            P("segment", "groups", None, "inner"),
            P("segment", "groups", None, "inner"),
        ),
        check_vma=False,
    )
```

```python
import functools

import jax
import jax.numpy as jnp
from jax import lax
from jax.experimental import pallas as pl
from jax.experimental.pallas import tpu as pltpu
from jax.sharding import PartitionSpec as P

EPS = 1e-05
MESH = pl.DeviceIdType.MESH
F32 = jnp.float32
BF16 = jnp.bfloat16


def column_of(row, first, count):
    length = row.shape[1]
    down = lax.broadcasted_iota(jnp.int32, (count, length), 0) + first
    across = lax.broadcasted_iota(jnp.int32, (count, length), 1)
    picked = jnp.where(down == across, jnp.broadcast_to(row, (count, length)), 0.0)
    return jnp.sum(picked, axis=1, keepdims=True)


def kernel(
    pieces, inner, segments,
    tokens_h, norm_gain_h, final_gain_h, taps_h, rate_h, residue_h,
    embedding, w_in, w_out, fir_state, modal_state, unembed,
    packed_out, fir_new, modal_new,
    product_v, tokens, norm_gain, final_gain, taps, rate, residue,
    emb_v, in_v, out_v, fir_v, modal_v, unembed_v,
    xbuf, fbuf, abuf, arbuf, bbuf, brbuf, zbuf, acc, mixed, squares, state_part, coefs, gated,
    head_acc, scatter, lbuf, ebuf,
    out_state_sem, small_sem, emb_sem, in_sem, out_sem, state_sem, unembed_sem,
    x_send, x_recv, a_send, a_recv, b_send, b_recv, z_send, f_send, f_recv,
    l_send, l_recv, e_send, e_recv,
):
    seg = lax.axis_index("segment")
    me = lax.axis_index("inner")
    last = segments - 1
    chips = inner // 2
    chip = me // 2
    core = me % 2
    steps = tokens.shape[0] - 1
    seqs = tokens.shape[1]
    rows = steps * seqs
    width = emb_v.shape[1]
    sub = width // pieces
    vocab = emb_v.shape[0]
    vocab_local = unembed.shape[1]
    padded = lbuf.shape[2]
    block = seqs // segments
    depth = fir_v.shape[0]
    full = inner * width
    is_short = seg % 2 == 0
    sibling = chip * 2 + (core + 1) % 2

    def member(dx, dc):
        return (chip + dx) % chips * 2 + (core + dc) % 2

    def remote(src, dst, send, recv, where):
        return pltpu.make_async_remote_copy(
            src_ref=src, dst_ref=dst, send_sem=send, recv_sem=recv,
            device_id=where, device_id_type=MESH,
        )

    def arrival(ref, sem):
        pltpu.make_async_copy(ref, ref, sem).wait()

    barrier = pltpu.get_barrier_semaphore()
    for p in range(1, inner):
        pl.semaphore_signal(
            barrier, inc=1, device_id={"inner": member(p // 2, p % 2)}, device_id_type=MESH
        )
    for d in range(1, segments):
        pl.semaphore_signal(
            barrier, inc=1, device_id={"segment": (seg + d) % segments}, device_id_type=MESH
        )

    emb_copy = pltpu.make_async_copy(embedding, emb_v, emb_sem)
    fir_copy = pltpu.make_async_copy(fir_state.at[0], fir_v, state_sem.at[0])
    modal_copy = pltpu.make_async_copy(modal_state.at[0], modal_v, state_sem.at[1])
    unembed_copy = pltpu.make_async_copy(unembed, unembed_v, unembed_sem)
    small = [
        pltpu.make_async_copy(source, target, small_sem.at[index])
        for index, (source, target) in enumerate((
            (tokens_h, tokens), (taps_h, taps), (rate_h, rate), (residue_h, residue),
            (norm_gain_h, norm_gain), (final_gain_h, final_gain),
        ))
    ]

    def in_copy(q, j):
        return pltpu.make_async_copy(
            w_in.at[0, j, pl.ds(pl.multiple_of(q * width, width), width), :],
            in_v.at[q, j],
            in_sem.at[q * 3 + j],
        )

    def out_copy(q, k):
        return pltpu.make_async_copy(
            w_out.at[0, :, pl.ds(pl.multiple_of(q * width + k * sub, sub), sub)],
            out_v.at[q * pieces + k],
            out_sem.at[q * pieces + k],
        )

    small[0].start()

    @pl.when(seg == 0)
    def _():
        emb_copy.start()

    for copy in small[1:]:
        copy.start()

    @pl.when(is_short)
    def _():
        fir_copy.start()

    @pl.when(jnp.logical_not(is_short))
    def _():
        modal_copy.start()

    for t in range(inner):
        for j in range(3):
            in_copy(member(t % chips, t // chips), j).start()

    @pl.loop(0, pieces * inner)
    def _(t):
        out_copy(member(t % chips, (t // chips + 1) % 2), t // inner).start()

    unembed_copy.start()

    @pl.when(is_short)
    def _():
        modal_copy.start()

    @pl.when(jnp.logical_not(is_short))
    def _():
        fir_copy.start()

    fir_whole = pltpu.make_async_copy(fir_v, fir_new, out_state_sem.at[0])
    fir_shift = pltpu.make_async_copy(
        fir_v.at[pl.ds(steps, depth - steps)],
        fir_new.at[pl.ds(0, depth - steps)],
        out_state_sem.at[0],
    )
    fir_latest = pltpu.make_async_copy(
        product_v, fir_new.at[pl.ds(depth - steps, steps)], out_state_sem.at[1]
    )
    modal_done = pltpu.make_async_copy(modal_v, modal_new, out_state_sem.at[2])

    small[0].wait()

    def gather_copy(buf, source, send, recv, k, dx):
        where = sibling if dx == 0 else member(dx, 0)
        return remote(
            source, buf.at[me * pieces + k], send.at[dx * pieces + k],
            recv.at[me * pieces + k], {"inner": where},
        )

    def hand_on(buf, send, recv, k, dx):
        q = member(dx, 0)
        return remote(
            buf.at[q * pieces + k], buf.at[q * pieces + k],
            send.at[(chips + dx) * pieces + k], recv.at[q * pieces + k], {"inner": sibling},
        )

    def x_copy(k, dx):
        return gather_copy(xbuf, xbuf.at[me * pieces + k], x_send, x_recv, k, dx)

    def f_copy(k, dx):
        return gather_copy(fbuf, zbuf.at[k], f_send, f_recv, k, dx)

    def spread(copy_of, k):
        for dx in range(chips - 1, -1, -1):
            copy_of(k, dx).start()

    def pass_on(buf, send, recv):
        for k in range(pieces):
            for dx in range(1, chips):
                q = member(dx, 0)
                arrival(buf.at[q * pieces + k], recv.at[q * pieces + k])
                hand_on(buf, send, recv, k, dx).start()

    @pl.when(seg == 0)
    def _():
        ids = jnp.concatenate(
            [column_of(tokens[pl.ds(t, 1), :].astype(F32), 0, seqs) for t in range(steps)], axis=0
        ).astype(jnp.int32)
        hot = lax.broadcasted_iota(jnp.int32, (rows, vocab), 1) == ids
        hot = hot.astype(F32).astype(BF16)
        emb_copy.wait()
        for k in range(pieces):
            looked_up = jnp.dot(
                hot, emb_v[:, k * sub:(k + 1) * sub], preferred_element_type=F32
            )
            xbuf[me * pieces + k] = looked_up.astype(BF16)

    pl.semaphore_wait(barrier, inner - 1 + segments - 1)

    @pl.when(seg == 0)
    def _():
        for k in range(pieces):
            spread(x_copy, k)

    for copy in small[1:]:
        copy.wait()

    acc[...] = jnp.zeros_like(acc)
    squares[...] = jnp.zeros_like(squares)

    @pl.when(is_short)
    def _():
        fir_copy.wait()
        for t in range(steps):
            coefs[t] = taps[t] if t <= depth else jnp.zeros((1, width), F32)
            for c in range(0, width, 256):
                cols = slice(c, c + 256)
                total = jnp.zeros((seqs, 256), F32)
                for i in range(depth - t):
                    total = total + fir_v[i + t, :, cols] * taps[depth - i, :, cols]
                state_part[t, :, cols] = total

    @pl.when(jnp.logical_not(is_short))
    def _():
        fir_copy.wait()
        fir_whole.start()
        decay = jnp.exp(-rate[0])
        weight = residue[0] * (1.0 - decay)
        for t in range(steps):
            coef = jnp.sum(weight, axis=0, keepdims=True)
            coefs[t] = coef + taps[0] if t == 0 else coef
            weight = weight * decay
        modal_copy.wait()

        @pl.loop(0, seqs)
        def _(b):
            value = modal_v[b]
            for t in range(steps):
                value = value * decay
                state_part[t, pl.ds(b, 1), :] = jnp.sum(value * residue[0], axis=0, keepdims=True)

    def take(values, gain):
        values = values.astype(F32)
        total = squares[...]
        for c in range(0, values.shape[1], 128):
            piece = values[:, c:c + 128]
            total = total + piece * piece
        squares[...] = total
        return (values * gain).astype(BF16)

    def block_of(buf, q):
        return jnp.concatenate([buf[q * pieces + k] for k in range(pieces)], axis=1)

    @pl.when(seg > 0)
    def _():
        for k in range(pieces):
            arrival(xbuf.at[me * pieces + k], x_recv.at[me * pieces + k])
            spread(x_copy, k)

    @pl.loop(0, inner)
    def _(t):
        q = member(t % chips, t // chips)

        @pl.when(t == 1)
        def _():
            pass_on(xbuf, x_send, x_recv)

        @pl.when(t >= chips)
        def _():
            for k in range(pieces):
                arrival(xbuf.at[q * pieces + k], x_recv.at[q * pieces + k])

        offset = pl.multiple_of(q * width, width)
        scaled = take(block_of(xbuf, q), norm_gain[:, pl.ds(offset, width)])
        for j in range(3):
            in_copy(q, j).wait()
            acc[j] += jnp.dot(scaled, in_v[q, j], preferred_element_type=F32)

    scale = lax.rsqrt(jnp.sum(squares[...], axis=1, keepdims=True) / full + EPS)
    for c in range(0, width, sub):
        cols = slice(c, c + sub)
        products = []
        for t in range(steps):
            part = slice(t * seqs, (t + 1) * seqs)
            scale_t = scale[part]
            product = (acc[1, part, cols] * scale_t) * (acc[2, part, cols] * scale_t)
            products.append(product)
            product_v[t, :, cols] = product
            filtered = state_part[t, :, cols]
            for u in range(t + 1):
                filtered = filtered + coefs[t - u, :, cols] * products[u]
            gated[part, cols] = (acc[0, part, cols] * scale_t * filtered).astype(BF16)

    def a_copy(k):
        return remote(abuf.at[k], arbuf.at[k], a_send.at[k], a_recv.at[k], {"inner": sibling})

    def b_copy(k, dx):
        return remote(
            bbuf.at[dx * pieces + k], brbuf.at[chip * pieces + k], b_send.at[dx * pieces + k],
            b_recv.at[chip * pieces + k], {"inner": member(dx, 0)},
        )

    def z_copy(k):
        return remote(
            zbuf.at[k], xbuf.at[me * pieces + k], z_send.at[k],
            x_recv.at[me * pieces + k], {"segment": (seg + 1) % segments},
        )

    def mix(q, k):
        out_copy(q, k).wait()
        return jnp.dot(gated[...], out_v[q * pieces + k], preferred_element_type=F32)

    @pl.loop(0, pieces)
    def _(k):
        @pl.loop(0, chips)
        def _(x):
            abuf[k, x] = mix(x * 2 + (core + 1) % 2, k).astype(BF16)

        a_copy(k).start()

    @pl.loop(0, pieces)
    def _(k):
        for dx in range(chips - 1, -1, -1):
            mixed[dx] = mix(member(dx, 0), k)
        arrival(arbuf.at[k], a_recv.at[k])
        for dx in range(chips - 1, 0, -1):
            total = mixed[dx] + arbuf[k, (chip + dx) % chips].astype(F32)
            bbuf[dx * pieces + k] = total.astype(BF16)
            b_copy(k, dx).start()
        total = mixed[0] + arbuf[k, chip].astype(F32)
        acc[0, :, pl.ds(pl.multiple_of(k * sub, sub), sub)] = (
            total + xbuf[me * pieces + k].astype(F32)
        )

    @pl.loop(0, pieces)
    def _(k):
        total = acc[0, :, pl.ds(pl.multiple_of(k * sub, sub), sub)]
        for dx in range(1, chips):
            source = (chip + dx) % chips * pieces + k
            arrival(brbuf.at[source], b_recv.at[source])
            total = total + brbuf[source].astype(F32)
        zbuf[k] = total.astype(BF16)

        @pl.when(seg < last)
        def _():
            z_copy(k).start()

        @pl.when(seg == last)
        def _():
            spread(f_copy, k)

    def finish_states():
        @pl.when(is_short)
        def _():
            fir_shift.start()
            fir_latest.start()
            modal_copy.wait()

        @pl.when(jnp.logical_not(is_short))
        def _():
            decay = jnp.exp(-rate[0])

            @pl.loop(0, seqs)
            def _(b):
                value = modal_v[b]
                for t in range(steps):
                    value = decay * value + (1.0 - decay) * product_v[t, pl.ds(b, 1), :]
                modal_v[b] = value

        modal_done.start()

    unembed_copy.wait()

    def l_copy(s):
        return remote(scatter.at[s], lbuf, l_send.at[s], l_recv, {"segment": s})

    @pl.when(seg == last)
    def _():
        squares[...] = jnp.zeros_like(squares)
        head_acc[...] = jnp.zeros_like(head_acc)

        def head(values, q):
            offset = pl.multiple_of(q * width, width)
            scaled = take(values, final_gain[:, pl.ds(offset, width)])
            head_acc[:, :vocab_local] += jnp.dot(
                scaled, unembed_v[pl.ds(offset, width), :], preferred_element_type=F32
            )

        head(jnp.concatenate([zbuf[k] for k in range(pieces)], axis=1), me)
        pass_on(fbuf, f_send, f_recv)

        @pl.loop(1, inner)
        def _(t):
            q = member(t % chips, t // chips)

            @pl.when(t >= chips)
            def _():
                for k in range(pieces):
                    arrival(fbuf.at[q * pieces + k], f_recv.at[q * pieces + k])

            head(block_of(fbuf, q), q)

        final_scale = lax.rsqrt(jnp.sum(squares[...], axis=1, keepdims=True) / full + EPS)
        logits = head_acc[...] * final_scale
        for s in range(segments):
            for t in range(steps):
                start = t * seqs + s * block
                if s < last:
                    scatter[s, t] = logits[start:start + block]
                else:
                    lbuf[t] = logits[start:start + block]
            if s < last:
                l_copy(s).start()

    @pl.when(seg < last)
    def _():
        finish_states()
        arrival(lbuf, l_recv)

    def e_copy(p):
        return remote(
            ebuf.at[me], ebuf.at[me], e_send.at[p], e_recv.at[me],
            {"inner": member(p // 2, p % 2)},
        )

    columns = lax.broadcasted_iota(jnp.int32, (block, vocab_local), 1) + me * vocab_local
    lanes = lax.broadcasted_iota(jnp.int32, (block, 128), 1)
    for t in range(steps):
        logits_t = lbuf[t, :, :vocab_local]
        packed_out[t, :, :vocab_local] = logits_t
        target = column_of(tokens[pl.ds(t + 1, 1), :].astype(F32), seg * block, block)
        hit = columns == target.astype(jnp.int32)
        exp_sum = jnp.sum(jnp.exp(logits_t), axis=1, keepdims=True)
        target_part = jnp.sum(jnp.where(hit, logits_t, 0.0), axis=1, keepdims=True)
        ebuf[me, t] = jnp.where(lanes == 0, exp_sum, target_part)
    for p in range(inner - 1, 0, -1):
        e_copy(p).start()

    @pl.when(seg == last)
    def _():
        finish_states()

    sums = ebuf[me]
    for p in range(1, inner):
        q = member(p // 2, p % 2)
        arrival(ebuf.at[q], e_recv.at[q])
        sums = sums + ebuf[q]
    for t in range(steps):
        logprob = sums[t, :, 1:2] - jnp.log(sums[t, :, 0:1])
        packed_out[t, :, padded:] = jnp.broadcast_to(logprob, (block, 128))

    @pl.when(is_short)
    def _():
        fir_shift.wait()
        fir_latest.wait()

    @pl.when(jnp.logical_not(is_short))
    def _():
        fir_whole.wait()

    modal_done.wait()

    @pl.loop(0, pieces)
    def _(k):
        a_copy(k).wait_send()
        for dx in range(chips):
            x_copy(k, dx).wait_send()
            if dx > 0:
                hand_on(xbuf, x_send, x_recv, k, dx).wait_send()
                b_copy(k, dx).wait_send()

        @pl.when(seg < last)
        def _():
            z_copy(k).wait_send()

        @pl.when(seg == last)
        def _():
            for dx in range(chips):
                f_copy(k, dx).wait_send()
                if dx > 0:
                    hand_on(fbuf, f_send, f_recv, k, dx).wait_send()

    @pl.when(seg == last)
    def _():
        for s in range(segments - 1):
            l_copy(s).wait_send()

    for p in range(1, inner):
        e_copy(p).wait_send()


def hand_out(
    vocab_local, padded, packed, fir_new, modal_new, logits, logprob, fir, modal,
    packed_v, logits_v, logprob_v, fir_v, modal_v, in_sems, out_sems,
):
    half = fir_v.shape[0] // 2
    share = modal_v.shape[0] // 2
    parts = [(fir_new, fir_v, fir, pl.ds(i * half, half)) for i in range(2)]
    parts += [(modal_new, modal_v, modal, pl.ds(i * share, share)) for i in range(2)]
    packed_copy = pltpu.make_async_copy(packed, packed_v, in_sems.at[4])
    logits_copy = pltpu.make_async_copy(logits_v, logits, out_sems.at[4])
    logprob_copy = pltpu.make_async_copy(logprob_v, logprob, out_sems.at[5])
    arriving = [
        pltpu.make_async_copy(source.at[where], held.at[where], in_sems.at[i])
        for i, (source, held, _, where) in enumerate(parts)
    ]
    leaving = [
        pltpu.make_async_copy(held.at[where], target.at[0, where], out_sems.at[i])
        for i, (_, held, target, where) in enumerate(parts)
    ]
    packed_copy.start()
    for copy in arriving:
        copy.start()
    packed_copy.wait()
    steps, block = logprob.shape
    down = lax.broadcasted_iota(jnp.int32, (block, block), 0)
    across = lax.broadcasted_iota(jnp.int32, (block, block), 1)
    for t in range(steps):
        logits_v[t] = packed_v[t, :, :vocab_local]
        spread_out = packed_v[t, :, padded:padded + block]
        logprob_v[t:t + 1, :] = jnp.sum(
            jnp.where(down == across, spread_out, 0.0), axis=0, keepdims=True
        )
    logits_copy.start()
    logprob_copy.start()
    for before, after in zip(arriving, leaving):
        before.wait()
        after.start()
    for copy in leaving:
        copy.wait()
    logits_copy.wait()
    logprob_copy.wait()


def per_device(
    inner, segments, tokens, embedding, in_proj, out_proj, norm_gain, fir_taps, modal_rate,
    modal_residue, fir_state, modal_state, final_gain, unembed,
):
    steps = tokens.shape[0] - 1
    seqs = tokens.shape[1]
    rows = steps * seqs
    vocab, width = embedding.shape
    pieces = max(1, width // 256)
    sub = width // pieces
    chips = inner // 2
    full = inner * width
    vocab_local = unembed.shape[1]
    padded = max(128, vocab_local)
    block = seqs // segments
    whole = pl.BlockSpec(memory_space=pltpu.VMEM)
    in_hbm = pl.BlockSpec(memory_space=pltpu.HBM)
    dma = pltpu.SemaphoreType.DMA
    fir_by_tap = jnp.transpose(fir_state, (0, 2, 1, 3))
    operands = (
        tokens, norm_gain, final_gain[None], jnp.transpose(fir_taps, (1, 0, 2)), modal_rate,
        modal_residue, embedding, in_proj, out_proj, fir_by_tap, modal_state, unembed,
    )
    packed, fir_new, modal_new = pl.pallas_call(
        functools.partial(kernel, pieces, inner, segments),
        out_shape=(
            jax.ShapeDtypeStruct((steps, block, padded + 128), F32),
            jax.ShapeDtypeStruct(fir_by_tap.shape[1:], F32),
            jax.ShapeDtypeStruct(modal_state.shape[1:], F32),
        ),
        in_specs=[in_hbm] * len(operands),
        out_specs=(whole, in_hbm, in_hbm),
        scratch_shapes=[
            pltpu.VMEM((steps, seqs, width), F32),
            *[pltpu.VMEM(o.shape, o.dtype) for o in operands[:6]],
            pltpu.VMEM((vocab, width), BF16),
            pltpu.VMEM((inner, 3, width, width), BF16),
            pltpu.VMEM((inner * pieces, width, sub), BF16),
            pltpu.VMEM(fir_by_tap.shape[1:], F32),
            pltpu.VMEM(modal_state.shape[1:], F32),
            pltpu.VMEM((full, vocab_local), BF16),
            pltpu.VMEM((inner * pieces, rows, sub), BF16),
            pltpu.VMEM((inner * pieces, rows, sub), BF16),
            pltpu.VMEM((pieces, chips, rows, sub), BF16),
            pltpu.VMEM((pieces, chips, rows, sub), BF16),
            pltpu.VMEM((chips * pieces, rows, sub), BF16),
            pltpu.VMEM((chips * pieces, rows, sub), BF16),
            pltpu.VMEM((pieces, rows, sub), BF16),
            pltpu.VMEM((3, rows, width), F32),
            pltpu.VMEM((chips, rows, sub), F32),
            pltpu.VMEM((rows, 128), F32),
            pltpu.VMEM((steps, seqs, width), F32),
            pltpu.VMEM((steps, 1, width), F32),
            pltpu.VMEM((rows, width), BF16),
            pltpu.VMEM((rows, padded), F32),
            pltpu.VMEM((segments, steps, block, padded), F32),
            pltpu.VMEM((steps, block, padded), F32),
            pltpu.VMEM((inner, steps, block, 128), F32),
            dma((3,)),
            dma((6,)),
            dma,
            dma((inner * 3,)),
            dma((inner * pieces,)),
            dma((2,)),
            dma,
            dma((inner * pieces,)),
            dma((inner * pieces,)),
            dma((pieces,)),
            dma((pieces,)),
            dma((chips * pieces,)),
            dma((chips * pieces,)),
            dma((pieces,)),
            dma((inner * pieces,)),
            dma((inner * pieces,)),
            dma((segments,)),
            dma,
            dma((inner,)),
            dma((inner,)),
        ],
        compiler_params=pltpu.CompilerParams(
            collective_id=0, has_side_effects=True, vmem_limit_bytes=60 * 1024 * 1024
        ),
    )(*operands)
    logits, logprob, fir_out, modal_out = pl.pallas_call(
        functools.partial(hand_out, vocab_local, padded),
        out_shape=(
            jax.ShapeDtypeStruct((steps, block, vocab_local), F32),
            jax.ShapeDtypeStruct((steps, block), F32),
            jax.ShapeDtypeStruct(fir_by_tap.shape, F32),
            jax.ShapeDtypeStruct(modal_state.shape, F32),
        ),
        in_specs=[in_hbm] * 3,
        out_specs=(in_hbm,) * 4,
        scratch_shapes=[
            pltpu.VMEM(packed.shape, F32),
            pltpu.VMEM((steps, block, vocab_local), F32),
            pltpu.VMEM((steps, block), F32),
            pltpu.VMEM(fir_new.shape, F32),
            pltpu.VMEM(modal_new.shape, F32),
            dma((5,)),
            dma((6,)),
        ],
        compiler_params=pltpu.CompilerParams(vmem_limit_bytes=60 * 1024 * 1024),
    )(packed, fir_new, modal_new)
    return (logits, logprob, jnp.transpose(fir_out, (0, 2, 1, 3)), modal_out)


def solution(mesh):
    inner = mesh.shape["inner"]
    segments = mesh.shape["segment"]
    return jax.shard_map(
        functools.partial(per_device, inner, segments),
        mesh=mesh,
        in_specs=(
            P(None, "groups"),
            P(None, "inner"),
            P("segment", None, None, "inner"),
            P("segment", "inner", None),
            P("segment", None),
            P("segment", None, "inner"),
            P("segment", None, "inner"),
            P("segment", None, "inner"),
            P("segment", "groups", None, "inner"),
            P("segment", "groups", None, "inner"),
            P(),
            P(None, "inner"),
        ),
        out_specs=(
            P(None, ("groups", "segment"), "inner"),
            P(None, ("groups", "segment")),
            P("segment", "groups", None, "inner"),
            P("segment", "groups", None, "inner"),
        ),
        check_vma=False,
    )
```
